32 devices in a mesh: scenario: 2 (over y), site: 4 (over z), structur: 2 (over x), sub: 2 (over core).
Axes of the slice: x: 2, y: 2, z: 4, core: 2. Of those that a mesh axis runs over, the one named last changes fastest.
Arguments:
- tiles: bfloat16 [8, 8, 8, 256, 256], P(('site', 'structur'), None, 'sub'), may hold values from -0.046875 to 0.046875
- history: bfloat16 [16, 9, 256, 128], P(('scenario', 'site', 'structur')), parts along dimension 0, may hold values from -6 to 6
- self_inverse: bfloat16 [8, 256, 256], P(('site', 'structur')), may hold values from -0.375 to 0.375
- pair_src: int32 [8, 8], P(('site', 'structur')), may hold values from 0 to 7, as said below
- pair_delay: int32 [8, 8], P(('site', 'structur')), may hold values from 1 to 2
- strike_seg: int32 [256], P('scenario'), parts along dimension 0, may hold values from 0 to 2047
- waveform: float32 [4, 128], P('scenario'), parts along dimension 0, may hold values from -24 to 24
Outputs:
- currents: bfloat16 [16, 2, 256, 128], P(('scenario', 'site', 'structur')), parts along dimension 0
The draws below stay inside these ranges and needn't reach their ends.
There are 2 independent parts, one for each index of `scenario`. The reference program is written for one: setup_inputs(seed, part) draws one part's arguments, and reference() takes and returns one part's arrays. A program takes and returns all parts, laid end to end along the dimension named above; an argument that names none is the same for every part. Nothing has to cross between parts.
Inputs may be any that keep to these rules, and one draw needn't show every extreme that they name: The source block's site, pair_src // 2, differs from the observer block's site, b // 2, by at most one.
All inputs are finite; a program needn't handle non-finite values.
Results may differ from the reference program's by a relative error of at most 0.0051.
Values may be sent and summed in bfloat16 or wider, within the bound.
No kernel may reach another device: no remote copies, remote signals or barrier semaphores. Data moves between devices by JAX's collectives and lax.ppermute only.
A program may use at most 128 MiB of HBM per device.

```python
import jax
import jax.numpy as jnp
from jax import lax

S = 256
TAPS = 8
NEAR = 8
MAXD = 2
STRIKES = 128
HLEN = 9
SITE_BLOCKS = 2
SITES = 4
BLOCKS = 8


def draw_pair_src(key, part):
    key = jax.random.fold_in(key, 7)
    key_site, key_block = jax.random.split(key)
    blocks = jnp.arange(BLOCKS, dtype=jnp.int32)
    own_site = blocks // SITE_BLOCKS
    offset = jax.random.randint(key_site, (BLOCKS, NEAR), -1, 2)
    target = jnp.clip(own_site[:, None] + offset, 0, SITES - 1)
    within = jax.random.randint(key_block, (BLOCKS, NEAR), 0, SITE_BLOCKS)
    return (target * SITE_BLOCKS + within).astype(jnp.int32)


def touch_ends(entries, stream_key, low, high):
    longest = entries.shape.index(max(entries.shape))
    spots = []
    for shift in (0, 1):
        where = [jax.random.randint(jax.random.fold_in(stream_key, axis), (), 0, length) for axis, length in enumerate(entries.shape)]
        where[longest] = (where[longest] + shift) % entries.shape[longest]
        spots.append(tuple(where))
    return entries.at[spots[0]].set(low).at[spots[1]].set(high)


def shard_levels(stream_key, shape, shards, smallest, high):
    def one(position, shards_of):
        draws = jax.random.uniform(jax.random.fold_in(jax.random.fold_in(stream_key, 6), position), (shards_of,), jnp.float32, smallest / len(shards), high / len(shards))
        return jnp.repeat(jnp.exp(draws), shape[position] // shards_of).reshape((-1,) + (1,) * (len(shape) - position - 1))

    level = one(*shards[0])
    for cut in shards[1:]:
        level = level * one(*cut)
    return level


def gaussian(rng, extent, deviation, limit, cuts=(), held_as=jnp.bfloat16):
    result = jax.random.normal(rng, extent, jnp.float32) * deviation
    if len(cuts) > 0:
        result = shard_levels(rng, extent, cuts, -0.22, 0.18) * result
    return jnp.clip(result, min=-limit, max=limit).astype(held_as)


def setup_inputs(seed: int = 0, part: int = 0) -> dict:
    key_of = jax.random.split(jax.random.key(seed), 8)
    own_keys = jax.random.split(jax.random.fold_in(key_of[7], part), 8)
    tiles = gaussian(key_of[0], (BLOCKS, NEAR, TAPS, S, S), (S * NEAR * TAPS) ** -0.5, 0.046875, ((0, 8), (2, 2)))
    history = gaussian(own_keys[1], (BLOCKS, HLEN, S, STRIKES), 1.0, 6.0, ((0, 8),))
    self_inverse = gaussian(key_of[2], (BLOCKS, S, S), S ** -0.5, 0.375, ((0, 8),))
    pair_src = draw_pair_src(jax.random.fold_in(key_of[7], 71), part)
    pair_delay = touch_ends(jax.random.randint(key_of[4], (BLOCKS, NEAR), 1, MAXD + 1), jax.random.fold_in(key_of[4], 1), 1, MAXD).astype(jnp.int32)
    strike_seg = touch_ends(jax.random.randint(own_keys[5], (STRIKES,), 0, BLOCKS * S), jax.random.fold_in(own_keys[5], 1), 0, (BLOCKS * S) - 1).astype(jnp.int32)
    waveform = gaussian(own_keys[6], (2, STRIKES), 4.0, 24.0, (), jnp.float32)
    return {"tiles": tiles, "history": history, "self_inverse": self_inverse, "pair_src": pair_src, "pair_delay": pair_delay, "strike_seg": strike_seg, "waveform": waveform}


def reference(tiles, history, self_inverse, pair_src, pair_delay, strike_seg, waveform):
    taps = jnp.arange(TAPS, dtype=jnp.int32)
    segs = jnp.arange(S, dtype=jnp.int32)

    def solve_block(args, step, newest):
        block, tile_b, inverse_b, src_b, delay_b = args
        back = delay_b[:, None] + taps[None, :] - 1 - step
        older = history[src_b[:, None], jnp.maximum(back, 0)]
        if step == 1:
            fresh = newest[src_b][:, None]
            older = jnp.where((back < 0)[:, :, None, None], fresh, older)
        field = jnp.einsum("pkij,pkjs->is", tile_b.astype(jnp.float32), older.astype(jnp.float32))
        hit = (block * S + segs)[:, None] == strike_seg[None, :]
        incident = jnp.where(hit, waveform[step][None, :], jnp.float32(0.0))
        rhs = (incident - field).astype(jnp.bfloat16)
        return jnp.dot(inverse_b, rhs, preferred_element_type=jnp.float32).astype(jnp.bfloat16)

    blocks = jnp.arange(BLOCKS, dtype=jnp.int32)
    pack = (blocks, tiles, self_inverse, pair_src, pair_delay)
    first = lax.map(lambda a: solve_block(a, 0, None), pack)
    second = lax.map(lambda a: solve_block(a, 1, first), pack)
    return jnp.stack([first, second], axis=1)
```

```python
import functools

import jax
import jax.numpy as jnp
from jax import lax
from jax.experimental import pallas as pl
from jax.experimental.pallas import tpu as pltpu
from jax.sharding import PartitionSpec as P

GRID_AXES = ("site", "structur", "sub")


def partner_site(site, kind, sites):
    other = site ^ 1 if kind == "even" else (site + 1 if site % 2 else site - 1)
    return other if 0 <= other < sites else None


def link_pairs(kind, turn, sites, groups):
    pairs = []
    for site in range(sites):
        to_site = site if kind == "own" else partner_site(site, kind, sites)
        if to_site is None:
            continue
        for member in range(groups):
            pairs.append(
                (site * groups + member, to_site * groups + (member - turn) % groups)
            )
    return pairs


def swap_cores(x):
    return lax.ppermute(x, "sub", [(0, 1), (1, 0)])


def field_kernel(first, count, has_acc, *refs):
    meta, tiles, extra = refs[:3]
    sources = refs[3 : 3 + count]
    refs = refs[3 + count :]
    acc_in = None
    if has_acc:
        acc_in, refs = refs[0], refs[1:]
    out, tile_buf, extra_buf, plane_buf, tile_sem, extra_sem, plane_sem = refs
    pairs, taps = tiles.shape[0], tiles.shape[1]
    planes = sources[0].shape[0]
    width = sources[0].shape[2]

    def wanted(p):
        slot = meta[0, p]
        return jnp.logical_and(slot >= first, slot < first + count)

    def tile_copy(p):
        return pltpu.make_async_copy(tiles.at[p], tile_buf.at[p], tile_sem.at[p])

    def extra_copy(p):
        return pltpu.make_async_copy(extra.at[p], extra_buf.at[p], extra_sem.at[p])

    def plane_copy(n):
        return pltpu.make_async_copy(
            sources[n], plane_buf.at[n, pl.ds(1, planes)], plane_sem.at[n]
        )

    for n in range(count):
        plane_copy(n).start()
    for p in range(pairs):

        @pl.when(wanted(p))
        def _():
            tile_copy(p).start()

        @pl.when(jnp.logical_and(wanted(p), meta[2, p] == 1))
        def _():
            extra_copy(p).start()

    for n in range(count):
        plane_buf[n, 0] = jnp.zeros(plane_buf.shape[2:], plane_buf.dtype)
    if has_acc:
        out[...] = acc_in[...]
    else:
        out[...] = jnp.zeros_like(out)
    for n in range(count):
        plane_copy(n).wait()

    for p in range(pairs):

        @pl.when(wanted(p))
        def _():
            slot = meta[0, p] - first
            late = meta[1, p]
            tile_copy(p).wait()
            total = None
            for k in range(taps):
                both = jnp.concatenate(
                    [plane_buf[slot, late + k + 1], plane_buf[slot, late + k]], axis=1
                )
                term = jnp.dot(
                    tile_buf[p, k], both, preferred_element_type=jnp.float32
                )
                total = term if total is None else total + term
            out[0] += total[:, :width]
            out[1] += total[:, width:]

        @pl.when(jnp.logical_and(wanted(p), meta[2, p] == 1))
        def _():
            extra_copy(p).wait()
            out[1] += jnp.dot(
                extra_buf[p],
                plane_buf[meta[0, p] - first, taps],
                preferred_element_type=jnp.float32,
            )


def field_part(meta, tiles, extra, sources, first, acc=None):
    count = len(sources)
    pairs, taps, rows, cols = tiles.shape
    planes, _, width = sources[0].shape
    anywhere = pl.BlockSpec(memory_space=pl.ANY)
    vmem = pl.BlockSpec(memory_space=pltpu.VMEM)
    operands = [meta, tiles, extra, *sources]
    specs = [pl.BlockSpec(memory_space=pltpu.SMEM)] + [anywhere] * (2 + count)
    if acc is not None:
        operands.append(acc)
        specs.append(vmem)
    plane_bytes = rows * width * 2
    need = (
        pairs * (taps + 1) * rows * cols * 2
        + count * (planes + 1) * plane_bytes
        + 16 * plane_bytes
    )
    return pl.pallas_call(
        functools.partial(field_kernel, first, count, acc is not None),
        out_shape=jax.ShapeDtypeStruct((2, rows, width), jnp.float32),
        in_specs=specs,
        out_specs=vmem,
        scratch_shapes=[
            pltpu.VMEM((pairs, taps, rows, cols), tiles.dtype),
            pltpu.VMEM((pairs, rows, cols), tiles.dtype),
            pltpu.VMEM((count, planes + 1, rows, width), sources[0].dtype),
            pltpu.SemaphoreType.DMA((pairs,)),
            pltpu.SemaphoreType.DMA((pairs,)),
            pltpu.SemaphoreType.DMA((count,)),
        ],
        compiler_params=pltpu.CompilerParams(vmem_limit_bytes=need + (2 << 20)),
        name="field_part",
    )(*operands)


def solve_rows(base, mine, other, inverse, strike, wave):
    rows, width = mine.shape
    segments = base + lax.broadcasted_iota(jnp.int32, (rows, width), 0)
    incident = jnp.where(segments == strike, wave, jnp.float32(0.0))
    rhs = (incident - (mine + other)).astype(jnp.bfloat16)
    return jnp.dot(inverse, rhs, preferred_element_type=jnp.float32).astype(
        jnp.bfloat16
    )


def first_kernel(meta, mine, other, inverse, strike, wave, out):
    out[...] = solve_rows(
        meta[3, 0], mine[...], other[...], inverse[...], strike[...], wave[0:1, :]
    )


def second_kernel(meta, first, mine, other, inverse, strike, wave, out):
    out[0] = first[...]
    out[1] = solve_rows(
        meta[3, 0], mine[...], other[...], inverse[...], strike[...], wave[1:2, :]
    )


def fresh_kernel(count, meta, tiles, extra, *refs):
    sources = refs[:count]
    acc, out, tile_buf, tile_sem = refs[count:]
    pairs = tiles.shape[0]

    def use(p, n):
        return meta[4, p] == n

    for p in range(pairs):
        local = jnp.logical_and(meta[4, p] >= 0, meta[3, 1] == 0)
        swapped = jnp.logical_and(meta[4, p] >= 0, meta[3, 1] == 1)

        @pl.when(local)
        def _():
            pltpu.make_async_copy(
                tiles.at[p, 0], tile_buf.at[p], tile_sem.at[p]
            ).start()

        @pl.when(swapped)
        def _():
            pltpu.make_async_copy(extra.at[p], tile_buf.at[p], tile_sem.at[p]).start()

    out[...] = acc[...]
    for p in range(pairs):

        @pl.when(meta[4, p] >= 0)
        def _():
            pltpu.make_async_copy(extra.at[p], tile_buf.at[p], tile_sem.at[p]).wait()

        for n in range(count):

            @pl.when(use(p, n))
            def _():
                out[...] += jnp.dot(
                    tile_buf[p], sources[n][...], preferred_element_type=jnp.float32
                )


def per_device(tiles, history, self_inverse, pair_src, pair_delay, strike_seg, waveform):
    sites, groups = lax.axis_size("site"), lax.axis_size("structur")
    site, member, core = (lax.axis_index(a) for a in GRID_AXES)
    tiles, history, inverse = tiles[0], history[0], self_inverse[0]
    src, delay = pair_src[0], pair_delay[0]
    pairs, taps, rows, cols = tiles.shape
    width = history.shape[2]

    planes = lax.dynamic_slice_in_dim(history, core * taps, taps + 1, axis=0)
    extra = swap_cores(tiles[:, 0])

    def fetch(x, kind, turn):
        return lax.ppermute(
            x, ("site", "structur"), link_pairs(kind, turn, sites, groups)
        )

    own = [planes] + [fetch(planes, "own", t) for t in range(1, groups)]
    even = [fetch(planes, "even", 0)]
    odd = [fetch(planes, "odd", 0)]
    even += [fetch(x, "even", 0) for x in own[1:]]
    odd += [fetch(x, "odd", 0) for x in own[1:]]
    near = own + even[:1] + odd[:1]
    far = even[1:] + odd[1:]

    turn = (src % groups - member) % groups
    dist = src // groups - site
    is_even = jnp.where(site % 2 == 0, dist == 1, dist == -1)
    slot = jnp.where(
        dist == 0,
        turn,
        jnp.where(
            turn == 0,
            jnp.where(is_even, groups, groups + 1),
            jnp.where(is_even, groups + 1 + turn, 2 * groups + turn),
        ),
    )

    messages = [("odd", t) for t in range(groups)]
    messages += [("even", t) for t in range(groups)]
    messages += [("own", t) for t in range(1, groups)]
    if len(messages) % 2 == 0:
        messages.append(None)
    rounds = (len(messages) + 1) // 2
    number = jnp.where(
        dist == 0,
        2 * groups - 1 + turn,
        jnp.where(is_even, groups + turn, turn),
    )
    mine_round = jnp.where(number % 2 == core, number // 2, -1)
    own_here = jnp.where(core == 1, rounds, -1)
    mine_round = jnp.where(
        jnp.logical_and(dist == 0, turn == 0), own_here, mine_round
    )
    mine_round = jnp.where(delay == 1, mine_round, -1)

    base = (site * groups + member) * rows
    lane = jnp.arange(pairs, dtype=jnp.int32)
    meta = jnp.stack(
        [
            slot,
            delay - 1,
            jnp.logical_and(delay == 1, core == 0).astype(jnp.int32),
            jnp.where(lane == 0, base, core),
            mine_round,
        ]
    ).astype(jnp.int32)

    acc = field_part(meta, tiles, extra, near, 0)
    acc = field_part(meta, tiles, extra, far, groups + 2, acc)
    mine0, mine1 = acc[0], acc[1]

    strike = strike_seg[None, :]
    smem = pl.BlockSpec(memory_space=pltpu.SMEM)
    vmem = pl.BlockSpec(memory_space=pltpu.VMEM)
    anywhere = pl.BlockSpec(memory_space=pl.ANY)
    current0 = pl.pallas_call(
        first_kernel,
        out_shape=jax.ShapeDtypeStruct((rows, width), jnp.bfloat16),
        in_specs=[smem] + [vmem] * 5,
        out_specs=vmem,
        name="first_currents",
    )(meta, mine0, swap_cores(mine0), inverse, strike, waveform)

    fresh = []
    for r in range(rounds):
        perm = []
        for c in range(2):
            m = 2 * r + c
            if m < len(messages) and messages[m] is not None:
                kind, t = messages[m]
                perm += [
                    (2 * a + c, 2 * b + c)
                    for a, b in link_pairs(kind, t, sites, groups)
                ]
        fresh.append(lax.ppermute(current0, GRID_AXES, perm))
    fresh.append(current0)

    mine1 = pl.pallas_call(
        functools.partial(fresh_kernel, len(fresh)),
        out_shape=jax.ShapeDtypeStruct((rows, width), jnp.float32),
        in_specs=[smem, anywhere, anywhere] + [vmem] * (len(fresh) + 1),
        out_specs=vmem,
        scratch_shapes=[
            pltpu.VMEM((pairs, rows, cols), tiles.dtype),
            pltpu.SemaphoreType.DMA((pairs,)),
        ],
        name="fresh_part",
    )(meta, tiles, extra, *fresh, mine1)

    currents = pl.pallas_call(
        second_kernel,
        out_shape=jax.ShapeDtypeStruct((2, rows, width), jnp.bfloat16),
        in_specs=[smem] + [vmem] * 6,
        out_specs=vmem,
        name="second_currents",
    )(meta, current0, mine1, swap_cores(mine1), inverse, strike, waveform)
    return currents[None]


def solution(mesh):
    in_specs = (
        P(("site", "structur"), None, "sub", None, None),
        P(("scenario", "site", "structur"), None, None, None),
        P(("site", "structur"), None, None),
        P(("site", "structur"), None),
        P(("site", "structur"), None),
        P("scenario"),
        P("scenario", None),
    )
    out_specs = P(("scenario", "site", "structur"), None, None, None)
    return jax.shard_map(
        per_device, mesh=mesh, in_specs=in_specs, out_specs=out_specs, check_vma=False
    )
```

```python
import functools

import jax
import jax.numpy as jnp
from jax import lax
from jax.experimental import pallas as pl
from jax.experimental.pallas import tpu as pltpu
from jax.sharding import PartitionSpec as P

GRID_AXES = ("site", "structur", "sub")
SMEM = pl.BlockSpec(memory_space=pltpu.SMEM)
VMEM = pl.BlockSpec(memory_space=pltpu.VMEM)
ANY = pl.BlockSpec(memory_space=pl.ANY)
SMALL = pltpu.CompilerParams(vmem_limit_bytes=4 << 20)

SLOT, LATE, NEWS, ORDER, PLACE = range(5)
CHUNK = 4


def held(x):
    return pltpu.with_memory_space_constraint(x, pltpu.VMEM)


def far(x):
    return pltpu.with_memory_space_constraint(x, pltpu.HBM)


def table(x):
    return pltpu.with_memory_space_constraint(x, pltpu.SMEM)


def partner_site(site, kind, sites):
    other = site ^ 1 if kind == "even" else (site + 1 if site % 2 else site - 1)
    return other if 0 <= other < sites else None


def link_pairs(kind, turn, sites, groups):
    pairs = []
    for site in range(sites):
        to_site = site if kind == "own" else partner_site(site, kind, sites)
        if to_site is None:
            continue
        for member in range(groups):
            pairs.append(
                (site * groups + member, to_site * groups + (member - turn) % groups)
            )
    return pairs


def swap_cores(x):
    return lax.ppermute(x, "sub", [(0, 1), (1, 0)])


def start_kernel(slots, sites, groups, *refs):
    src, delay, history, tiles, planes, taps, meta, src_buf, delay_buf, sem = refs
    site, member, core = (lax.axis_index(a) for a in GRID_AXES)
    count, rows = planes.shape[:2]
    copies = [
        pltpu.make_async_copy(
            history.at[pl.ds(core * (count - 1), count)], planes, sem.at[0]
        ),
        pltpu.make_async_copy(src, src_buf, sem.at[1]),
        pltpu.make_async_copy(delay, delay_buf, sem.at[2]),
        pltpu.make_async_copy(tiles.at[:, 0], taps, sem.at[3]),
    ]
    for copy in copies:
        copy.start()
    copies[1].wait()
    copies[2].wait()
    even_step = jnp.where(site % 2 == 0, 1, -1)
    ahead = jnp.int32(0)
    behind = jnp.int32(src.shape[1])
    for p in range(src.shape[1]):
        value, wait = src_buf[0, p], delay_buf[0, p]
        turn = (value % groups - member + groups) % groups
        dist = value // groups - site
        kind = jnp.where(dist == 0, 2, jnp.where(dist == even_step, 1, 0))
        key = kind * groups + turn
        slot = jnp.int32(-1)
        for n in range(3 * groups):
            mine = jnp.where(core == 0, slots[0][n], slots[1][n])
            slot = jnp.where(key == n, mine, slot)
        mine = jnp.where(kind == 2, 0, jnp.where(kind == 1 - core, 1, -1))
        news = jnp.logical_and(wait == 1, mine >= 0)
        meta[SLOT, p] = slot
        meta[LATE, p] = wait - 1
        meta[NEWS, p] = jnp.where(news, 2 * turn + mine, -1)
        relayed = slot >= groups + 2
        behind = behind - jnp.where(relayed, 0, 1)
        meta[ORDER, jnp.where(relayed, ahead, behind)] = p
        ahead = ahead + jnp.where(relayed, 1, 0)
        meta[PLACE, p] = core
    meta[PLACE, 0] = (site * groups + member) * rows
    meta[PLACE, 2] = ahead
    copies[0].wait()
    copies[3].wait()


def near_kernel(count, meta, tiles, extra, *refs):
    sources, (total, newest) = refs[:count], refs[count:]
    width = sources[0].shape[2]
    taps = tiles.shape[1]
    core = meta[PLACE, 1]
    total[...] = jnp.zeros_like(total)

    def one(p, source):
        late = meta[LATE, p]
        empty = jnp.zeros(source.shape[1:], source.dtype)
        right = jnp.where(late == 1, source[0], empty)
        planes = []
        for k in range(taps):
            planes.append(jnp.concatenate([source[late + k], right], axis=1))
            right = source[late + k]
        total[...] += jnp.dot(
            jnp.concatenate([tiles[p, k] for k in range(taps)], axis=1),
            jnp.concatenate(planes, axis=0),
            preferred_element_type=jnp.float32,
        )

        @pl.when(jnp.logical_and(core == 0, late == 0))
        def _():
            total[:, width:] += jnp.dot(
                extra[p], source[taps - 1], preferred_element_type=jnp.float32
            )

    @pl.loop(0, tiles.shape[0])
    def _(p):
        @pl.when(core == 0)
        def _():
            newest[p] = tiles[p, 0]

        @pl.when(core == 1)
        def _():
            newest[p] = extra[p]

        for slot, source in enumerate(sources):
            pl.when(meta[SLOT, p] == slot)(functools.partial(one, p, source))


def near_part(meta, tiles, extra, sources):
    rows, width = sources[0].shape[1:]
    return pl.pallas_call(
        functools.partial(near_kernel, len(sources)),
        out_shape=[
            pltpu.VMEM((rows, 2 * width), jnp.float32),
            pltpu.VMEM(extra.shape, extra.dtype),
        ],
        in_specs=[SMEM] + [VMEM] * (2 + len(sources)),
        out_specs=[VMEM, VMEM],
        compiler_params=SMALL,
        name="near_part",
    )(table(meta), held(tiles), held(extra), *[held(x) for x in sources])


def relayed_kernel(first, count, meta, tiles, extra, acc, *refs):
    sources, (out0, out1, total, store) = refs[:count], refs[count:]
    planes, _, width = sources[0].shape
    pairs, taps = tiles.shape[:2]
    none = count * planes
    for n, source in enumerate(sources):
        store[n * planes : (n + 1) * planes] = source[...]
    store[none] = jnp.zeros(store.shape[1:], store.dtype)
    total[...] = acc[...]

    def chunk(start):
        numbers, left, right, swapped = [], [], [], []
        for i in range(start, start + CHUNK):
            p = meta[ORDER, i]
            used = i < meta[PLACE, 2]
            late = meta[LATE, p]
            base = (meta[SLOT, p] - first) * planes
            numbers.append(p)
            places = [jnp.where(used, base + late + k, none) for k in range(taps)]
            before = jnp.where(jnp.logical_and(used, late == 1), base, none)
            left += places
            right += [before] + places[:-1]
            swapped.append(
                jnp.where(jnp.logical_and(used, late == 0), base + taps - 1, none)
            )
        total[...] += jnp.dot(
            jnp.concatenate([tiles[p, k] for p in numbers for k in range(taps)], axis=1),
            jnp.concatenate(
                [
                    jnp.concatenate([store[a], store[b]], axis=1)
                    for a, b in zip(left, right)
                ],
                axis=0,
            ),
            preferred_element_type=jnp.float32,
        )

        @pl.when(meta[PLACE, 1] == 0)
        def _():
            total[:, width:] += jnp.dot(
                jnp.concatenate([extra[p] for p in numbers], axis=1),
                jnp.concatenate([store[a] for a in swapped], axis=0),
                preferred_element_type=jnp.float32,
            )

    for start in range(0, pairs, CHUNK):
        pl.when(meta[PLACE, 2] > start)(functools.partial(chunk, start))
    out0[...] = total[:, :width]
    out1[...] = total[:, width:]


def relayed_part(meta, tiles, extra, acc, sources, first):
    planes, rows, width = sources[0].shape
    store = (len(sources) * planes + 1, rows, width)
    half = pltpu.VMEM((rows, width), jnp.float32)
    room = 2 * store[0] * rows * width + 4 * acc.size
    return pl.pallas_call(
        functools.partial(relayed_kernel, first, len(sources)),
        out_shape=[half, half],
        in_specs=[SMEM] + [VMEM] * (3 + len(sources)),
        out_specs=[VMEM, VMEM],
        scratch_shapes=[
            pltpu.VMEM(acc.shape, acc.dtype),
            pltpu.VMEM(store, sources[0].dtype),
        ],
        compiler_params=pltpu.CompilerParams(vmem_limit_bytes=room + (4 << 20)),
        name="relayed_part",
    )(table(meta), held(tiles), held(extra), held(acc), *[held(x) for x in sources])


def solve_rows(base, mine, other, inverse, strike, wave):
    rows, width = mine.shape
    segments = base + lax.broadcasted_iota(jnp.int32, (rows, width), 0)
    incident = jnp.where(segments == strike, wave, jnp.float32(0.0))
    rhs = (incident - (mine + other)).astype(jnp.bfloat16)
    return jnp.dot(inverse, rhs, preferred_element_type=jnp.float32).astype(
        jnp.bfloat16
    )


def first_kernel(meta, mine, other, inverse, strike, wave, out):
    out[...] = solve_rows(
        meta[PLACE, 0], mine[...], other[...], inverse[...], strike[...], wave[0:1, :]
    )


def second_kernel(meta, first, mine, other, inverse, strike, wave, out):
    out[0] = first[...]
    out[1] = solve_rows(
        meta[PLACE, 0], mine[...], other[...], inverse[...], strike[...], wave[1:2, :]
    )


def pack_kernel(meta, own, other, out):
    half = own.shape[0] // 2

    @pl.when(meta[PLACE, 1] == 0)
    def _():
        out[:half] = own[:half]

    @pl.when(meta[PLACE, 1] == 1)
    def _():
        out[:half] = own[half:]

    out[half:] = other[...]


def pack(meta, own, other):
    rows, width = own.shape
    return pl.pallas_call(
        pack_kernel,
        out_shape=pltpu.VMEM((rows // 2 + rows, width), own.dtype),
        in_specs=[SMEM] + [VMEM] * 2,
        out_specs=VMEM,
        compiler_params=SMALL,
        name="pack",
    )(table(meta), held(own), held(other))


def fresh_kernel(turn, meta, tiles, source, acc, out):
    out[...] = acc[...]
    half = tiles.shape[2] // 2
    core = meta[PLACE, 1]

    def add(left, right):
        out[...] += jnp.dot(left, right, preferred_element_type=jnp.float32)

    @pl.loop(0, tiles.shape[0])
    def _(p):
        news = meta[NEWS, p]

        @pl.when(jnp.logical_and(news == 2 * turn, core == 0))
        def _():
            add(tiles[p, :, :half], source[:half])

        @pl.when(jnp.logical_and(news == 2 * turn, core == 1))
        def _():
            add(tiles[p, :, half:], source[:half])

        @pl.when(news == 2 * turn + 1)
        def _():
            add(tiles[p], source[half:])


def fresh_part(meta, tiles, source, turn, acc):
    return pl.pallas_call(
        functools.partial(fresh_kernel, turn),
        out_shape=pltpu.VMEM(acc.shape, acc.dtype),
        in_specs=[SMEM] + [VMEM] * 3,
        out_specs=VMEM,
        compiler_params=SMALL,
        name="fresh_part",
    )(table(meta), held(tiles), held(source), held(acc))


def per_device(tiles, history, self_inverse, pair_src, pair_delay, strike_seg, waveform):
    sites, groups = lax.axis_size("site"), lax.axis_size("structur")
    tiles, history, inverse = tiles[0], history[0], self_inverse[0]
    pairs, taps, rows, cols = tiles.shape
    width = history.shape[2]

    kinds = ("odd", "even", "own")
    key = {(k, t): n * groups + t for n, k in enumerate(kinds) for t in range(groups)}

    def send(x, *messages):
        pairs = [
            (2 * a + c, 2 * b + c)
            for c, m in enumerate(messages)
            for a, b in link_pairs(*m, sites, groups)
        ]
        return lax.ppermute(x, GRID_AXES, pairs)

    slots = [[-1] * (3 * groups) for _ in range(2)]
    for c in range(2):
        for t in range(groups):
            slots[c][key["own", t]] = t
            for n, kind in enumerate(("even", "odd")):
                slots[c][key[kind, t]] = groups + 2 * t + (n ^ c)

    planes, taps0, meta = pl.pallas_call(
        functools.partial(start_kernel, slots, sites, groups),
        out_shape=[
            pltpu.VMEM((taps + 1, rows, width), history.dtype),
            pltpu.VMEM((pairs, rows, cols), tiles.dtype),
            pltpu.SMEM((5, pairs), jnp.int32),
        ],
        in_specs=[ANY] * 4,
        out_specs=[VMEM, VMEM, SMEM],
        scratch_shapes=[
            pltpu.SMEM((1, pairs), jnp.int32),
            pltpu.SMEM((1, pairs), jnp.int32),
            pltpu.SemaphoreType.DMA((4,)),
        ],
        compiler_params=SMALL,
        name="start",
    )(far(pair_src), far(pair_delay), far(history), far(tiles))

    own = [planes] + [send(planes, *[("own", t)] * 2) for t in range(1, groups)]
    partners = []
    for x in own:
        partners.append(send(x, ("even", 0), ("odd", 0)))
        partners.append(send(x, ("odd", 0), ("even", 0)))
    extra = swap_cores(taps0)

    acc, newest = near_part(meta, tiles, extra, own + partners[:2])
    mine0, mine1 = relayed_part(meta, tiles, extra, acc, partners[2:], groups + 2)

    strike, inverse, wave = held(strike_seg[None, :]), held(inverse), held(waveform)
    current0 = pl.pallas_call(
        first_kernel,
        out_shape=pltpu.VMEM((rows, width), jnp.bfloat16),
        in_specs=[SMEM] + [VMEM] * 5,
        out_specs=VMEM,
        compiler_params=SMALL,
        name="first_currents",
    )(table(meta), held(mine0), held(swap_cores(mine0)), inverse, strike, wave)

    packed = pack(meta, current0, send(current0, ("even", 0), ("odd", 0)))
    passed = [send(packed, *[("own", t)] * 2) for t in range(1, groups)]
    for turn, block in enumerate([packed] + passed):
        mine1 = fresh_part(meta, newest, block, turn, mine1)

    currents = pl.pallas_call(
        second_kernel,
        out_shape=jax.ShapeDtypeStruct((2, rows, width), jnp.bfloat16),
        in_specs=[SMEM] + [VMEM] * 6,
        out_specs=VMEM,
        compiler_params=SMALL,
        name="second_currents",
    )(
        table(meta),
        held(current0),
        held(mine1),
        held(swap_cores(mine1)),
        inverse,
        strike,
        wave,
    )
    return currents[None]


def solution(mesh):
    in_specs = (
        P(("site", "structur"), None, "sub", None, None),
        P(("scenario", "site", "structur"), None, None, None),
        P(("site", "structur"), None, None),
        P(("site", "structur"), None),
        P(("site", "structur"), None),
        P("scenario"),
        P("scenario", None),
    )
    out_specs = P(("scenario", "site", "structur"), None, None, None)
    return jax.shard_map(
        per_device, mesh=mesh, in_specs=in_specs, out_specs=out_specs, check_vma=False
    )
```

```python
import functools

import jax
import jax.numpy as jnp
from jax import lax
from jax.experimental import pallas as pl
from jax.experimental.pallas import tpu as pltpu
from jax.sharding import PartitionSpec as P

GRID_AXES = ("site", "structur", "sub")
ALL_AXES = ("scenario",) + GRID_AXES
SMEM = pl.BlockSpec(memory_space=pltpu.SMEM)
VMEM = pl.BlockSpec(memory_space=pltpu.VMEM)
ANY = pl.BlockSpec(memory_space=pl.ANY)
SMALL = pltpu.CompilerParams(vmem_limit_bytes=4 << 20)

SLOT, LATE, NEWS, ORDER, PLACE = range(5)
CHUNK = 4


def held(x):
    return pltpu.with_memory_space_constraint(x, pltpu.VMEM)


def far(x):
    return pltpu.with_memory_space_constraint(x, pltpu.HBM)


def table(x):
    return pltpu.with_memory_space_constraint(x, pltpu.SMEM)


def partner_site(site, kind, sites):
    other = site ^ 1 if kind == "even" else (site + 1 if site % 2 else site - 1)
    return other if 0 <= other < sites else None


def link_pairs(kind, turn, sites, groups):
    pairs = []
    for site in range(sites):
        to_site = site if kind == "own" else partner_site(site, kind, sites)
        if to_site is None:
            continue
        for member in range(groups):
            pairs.append(
                (site * groups + member, to_site * groups + (member - turn) % groups)
            )
    return pairs


def swap_cores(x):
    return lax.ppermute(x, "sub", [(0, 1), (1, 0)])


def start_kernel(slots, sites, groups, *refs):
    src, delay, history, tiles, planes, taps, meta, src_buf, delay_buf, sem = refs
    site, member, core = (lax.axis_index(a) for a in GRID_AXES)
    count, rows = planes.shape[:2]
    copies = [
        pltpu.make_async_copy(
            history.at[pl.ds(core * (count - 1), count)], planes, sem.at[0]
        ),
        pltpu.make_async_copy(src, src_buf, sem.at[1]),
        pltpu.make_async_copy(delay, delay_buf, sem.at[2]),
        pltpu.make_async_copy(tiles.at[:, 0], taps, sem.at[3]),
    ]
    for copy in copies:
        copy.start()
    copies[1].wait()
    copies[2].wait()
    even_step = jnp.where(site % 2 == 0, 1, -1)
    ahead = jnp.int32(0)
    behind = jnp.int32(src.shape[1])
    for p in range(src.shape[1]):
        value, wait = src_buf[0, p], delay_buf[0, p]
        turn = (value % groups - member + groups) % groups
        dist = value // groups - site
        kind = jnp.where(dist == 0, 2, jnp.where(dist == even_step, 1, 0))
        key = kind * groups + turn
        slot = jnp.int32(-1)
        for n in range(3 * groups):
            mine = jnp.where(core == 0, slots[0][n], slots[1][n])
            slot = jnp.where(key == n, mine, slot)
        mine = jnp.where(kind == 2, 0, jnp.where(kind == 1 - core, 1, -1))
        news = jnp.logical_and(wait == 1, mine >= 0)
        meta[SLOT, p] = slot
        meta[LATE, p] = wait - 1
        meta[NEWS, p] = jnp.where(news, 2 * turn + mine, -1)
        relayed = slot >= groups + 2
        behind = behind - jnp.where(relayed, 0, 1)
        meta[ORDER, jnp.where(relayed, ahead, behind)] = p
        ahead = ahead + jnp.where(relayed, 1, 0)
        meta[PLACE, p] = core
    meta[PLACE, 0] = (site * groups + member) * rows
    meta[PLACE, 2] = ahead
    copies[0].wait()
    copies[3].wait()


def near_kernel(count, meta, tiles, extra, *refs):
    sources, (total, newest) = refs[:count], refs[count:]
    width = sources[0].shape[2]
    taps = tiles.shape[1]
    core = meta[PLACE, 1]
    total[...] = jnp.zeros_like(total)

    def one(p, source):
        late = meta[LATE, p]
        empty = jnp.zeros(source.shape[1:], source.dtype)
        right = jnp.where(late == 1, source[0], empty)
        planes = []
        for k in range(taps):
            planes.append(jnp.concatenate([source[late + k], right], axis=1))
            right = source[late + k]
        total[...] += jnp.dot(
            jnp.concatenate([tiles[p, k] for k in range(taps)], axis=1),
            jnp.concatenate(planes, axis=0),
            preferred_element_type=jnp.float32,
        )

        @pl.when(jnp.logical_and(core == 0, late == 0))
        def _():
            total[:, width:] += jnp.dot(
                extra[p], source[taps - 1], preferred_element_type=jnp.float32
            )

    @pl.loop(0, tiles.shape[0])
    def _(p):
        @pl.when(core == 0)
        def _():
            newest[p] = tiles[p, 0]

        @pl.when(core == 1)
        def _():
            newest[p] = extra[p]

        for slot, source in enumerate(sources):
            pl.when(meta[SLOT, p] == slot)(functools.partial(one, p, source))


def near_part(meta, tiles, extra, sources):
    rows, width = sources[0].shape[1:]
    return pl.pallas_call(
        functools.partial(near_kernel, len(sources)),
        out_shape=[
            pltpu.VMEM((rows, 2 * width), jnp.float32),
            pltpu.VMEM(extra.shape, extra.dtype),
        ],
        in_specs=[SMEM] + [VMEM] * (2 + len(sources)),
        out_specs=[VMEM, VMEM],
        compiler_params=SMALL,
        name="near_part",
    )(table(meta), held(tiles), held(extra), *[held(x) for x in sources])


def relayed_kernel(first, count, meta, tiles, extra, acc, *refs):
    sources, (out0, out1, total, store) = refs[:count], refs[count:]
    planes, _, width = sources[0].shape
    pairs, taps = tiles.shape[:2]
    none = count * planes
    for n, source in enumerate(sources):
        store[n * planes : (n + 1) * planes] = source[...]
    store[none] = jnp.zeros(store.shape[1:], store.dtype)
    total[...] = acc[...]

    def chunk(start):
        numbers, left, right, swapped = [], [], [], []
        for i in range(start, start + CHUNK):
            p = meta[ORDER, i]
            used = i < meta[PLACE, 2]
            late = meta[LATE, p]
            base = (meta[SLOT, p] - first) * planes
            numbers.append(p)
            places = [jnp.where(used, base + late + k, none) for k in range(taps)]
            before = jnp.where(jnp.logical_and(used, late == 1), base, none)
            left += places
            right += [before] + places[:-1]
            swapped.append(
                jnp.where(jnp.logical_and(used, late == 0), base + taps - 1, none)
            )
        total[...] += jnp.dot(
            jnp.concatenate([tiles[p, k] for p in numbers for k in range(taps)], axis=1),
            jnp.concatenate(
                [
                    jnp.concatenate([store[a], store[b]], axis=1)
                    for a, b in zip(left, right)
                ],
                axis=0,
            ),
            preferred_element_type=jnp.float32,
        )

        @pl.when(meta[PLACE, 1] == 0)
        def _():
            total[:, width:] += jnp.dot(
                jnp.concatenate([extra[p] for p in numbers], axis=1),
                jnp.concatenate([store[a] for a in swapped], axis=0),
                preferred_element_type=jnp.float32,
            )

    for start in range(0, pairs, CHUNK):
        pl.when(meta[PLACE, 2] > start)(functools.partial(chunk, start))
    out0[...] = total[:, :width]
    out1[...] = total[:, width:]


def relayed_part(meta, tiles, extra, acc, sources, first):
    planes, rows, width = sources[0].shape
    store = (len(sources) * planes + 1, rows, width)
    half = pltpu.VMEM((rows, width), jnp.float32)
    room = 2 * store[0] * rows * width + 4 * acc.size
    return pl.pallas_call(
        functools.partial(relayed_kernel, first, len(sources)),
        out_shape=[half, half],
        in_specs=[SMEM] + [VMEM] * (3 + len(sources)),
        out_specs=[VMEM, VMEM],
        scratch_shapes=[
            pltpu.VMEM(acc.shape, acc.dtype),
            pltpu.VMEM(store, sources[0].dtype),
        ],
        compiler_params=pltpu.CompilerParams(vmem_limit_bytes=room + (4 << 20)),
        name="relayed_part",
    )(table(meta), held(tiles), held(extra), held(acc), *[held(x) for x in sources])


def solve_rows(base, mine, other, inverse, strike, wave):
    rows, width = mine.shape
    segments = base + lax.broadcasted_iota(jnp.int32, (rows, width), 0)
    incident = jnp.where(segments == strike, wave, jnp.float32(0.0))
    rhs = (incident - (mine + other)).astype(jnp.bfloat16)
    return jnp.dot(inverse, rhs, preferred_element_type=jnp.float32).astype(
        jnp.bfloat16
    )


def first_kernel(meta, mine, other, inverse, strike, wave, out):
    out[...] = solve_rows(
        meta[PLACE, 0], mine[...], other[...], inverse[...], strike[...], wave[0:1, :]
    )


def second_kernel(meta, first, mine, other, inverse, strike, wave, out):
    out[0] = first[...]
    out[1] = solve_rows(
        meta[PLACE, 0], mine[...], other[...], inverse[...], strike[...], wave[1:2, :]
    )


def pack_kernel(meta, own, other, out):
    half = own.shape[0] // 2

    @pl.when(meta[PLACE, 1] == 0)
    def _():
        out[:half] = own[:half]

    @pl.when(meta[PLACE, 1] == 1)
    def _():
        out[:half] = own[half:]

    out[half:] = other[...]


def pack(meta, own, other):
    rows, width = own.shape
    return pl.pallas_call(
        pack_kernel,
        out_shape=pltpu.VMEM((rows // 2 + rows, width), own.dtype),
        in_specs=[SMEM] + [VMEM] * 2,
        out_specs=VMEM,
        compiler_params=SMALL,
        name="pack",
    )(table(meta), held(own), held(other))


def fresh_kernel(turn, meta, tiles, source, acc, out):
    out[...] = acc[...]
    half = tiles.shape[2] // 2
    core = meta[PLACE, 1]

    def add(left, right):
        out[...] += jnp.dot(left, right, preferred_element_type=jnp.float32)

    @pl.loop(0, tiles.shape[0])
    def _(p):
        news = meta[NEWS, p]

        @pl.when(jnp.logical_and(news == 2 * turn, core == 0))
        def _():
            add(tiles[p, :, :half], source[:half])

        @pl.when(jnp.logical_and(news == 2 * turn, core == 1))
        def _():
            add(tiles[p, :, half:], source[:half])

        @pl.when(news == 2 * turn + 1)
        def _():
            add(tiles[p], source[half:])


def fresh_part(meta, tiles, source, turn, acc):
    return pl.pallas_call(
        functools.partial(fresh_kernel, turn),
        out_shape=pltpu.VMEM(acc.shape, acc.dtype),
        in_specs=[SMEM] + [VMEM] * 3,
        out_specs=VMEM,
        compiler_params=SMALL,
        name="fresh_part",
    )(table(meta), held(tiles), held(source), held(acc))


def per_device(tiles, history, self_inverse, pair_src, pair_delay, strike_seg, waveform):
    sites, groups = lax.axis_size("site"), lax.axis_size("structur")
    tiles, history, inverse = tiles[0], history[0], self_inverse[0]
    pairs, taps, rows, cols = tiles.shape
    width = history.shape[2]

    kinds = ("odd", "even", "own")
    key = {(k, t): n * groups + t for n, k in enumerate(kinds) for t in range(groups)}

    def send(x, *messages):
        scenarios, grid = lax.axis_size("scenario"), sites * groups * 2
        pairs = []
        for scenario in range(scenarios):
            twin = scenario ^ 1
            for c, m in enumerate(messages):
                moves = dict(link_pairs(*m, sites, groups))
                for a in range(sites * groups):
                    source = scenario * grid + 2 * a + c
                    if a in moves:
                        pairs.append((source, scenario * grid + 2 * moves[a] + c))
                    elif twin < scenarios:
                        pairs.append((source, twin * grid + 2 * a + c))
        return lax.ppermute(x, ALL_AXES, pairs)

    slots = [[-1] * (3 * groups) for _ in range(2)]
    for c in range(2):
        for t in range(groups):
            slots[c][key["own", t]] = t
            for n, kind in enumerate(("even", "odd")):
                slots[c][key[kind, t]] = groups + 2 * t + (n ^ c)

    planes, taps0, meta = pl.pallas_call(
        functools.partial(start_kernel, slots, sites, groups),
        out_shape=[
            pltpu.VMEM((taps + 1, rows, width), history.dtype),
            pltpu.VMEM((pairs, rows, cols), tiles.dtype),
            pltpu.SMEM((5, pairs), jnp.int32),
        ],
        in_specs=[ANY] * 4,
        out_specs=[VMEM, VMEM, SMEM],
        scratch_shapes=[
            pltpu.SMEM((1, pairs), jnp.int32),
            pltpu.SMEM((1, pairs), jnp.int32),
            pltpu.SemaphoreType.DMA((4,)),
        ],
        compiler_params=SMALL,
        name="start",
    )(far(pair_src), far(pair_delay), far(history), far(tiles))

    own = [planes] + [send(planes, *[("own", t)] * 2) for t in range(1, groups)]
    partners = []
    for x in own:
        partners.append(send(x, ("even", 0), ("odd", 0)))
        partners.append(send(x, ("odd", 0), ("even", 0)))
    extra = swap_cores(taps0)

    acc, newest = near_part(meta, tiles, extra, own + partners[:2])
    mine0, mine1 = relayed_part(meta, tiles, extra, acc, partners[2:], groups + 2)

    strike, inverse, wave = held(strike_seg[None, :]), held(inverse), held(waveform)
    current0 = pl.pallas_call(
        first_kernel,
        out_shape=pltpu.VMEM((rows, width), jnp.bfloat16),
        in_specs=[SMEM] + [VMEM] * 5,
        out_specs=VMEM,
        compiler_params=SMALL,
        name="first_currents",
    )(table(meta), held(mine0), held(swap_cores(mine0)), inverse, strike, wave)

    packed = pack(meta, current0, send(current0, ("even", 0), ("odd", 0)))
    passed = [send(packed, *[("own", t)] * 2) for t in range(1, groups)]
    for turn, block in enumerate([packed] + passed):
        mine1 = fresh_part(meta, newest, block, turn, mine1)

    currents = pl.pallas_call(
        second_kernel,
        out_shape=jax.ShapeDtypeStruct((2, rows, width), jnp.bfloat16),
        in_specs=[SMEM] + [VMEM] * 6,
        out_specs=VMEM,
        compiler_params=SMALL,
        name="second_currents",
    )(
        table(meta),
        held(current0),
        held(mine1),
        held(swap_cores(mine1)),
        inverse,
        strike,
        wave,
    )
    return currents[None]


def solution(mesh):
    in_specs = (
        P(("site", "structur"), None, "sub", None, None),
        P(("scenario", "site", "structur"), None, None, None),
        P(("site", "structur"), None, None),
        P(("site", "structur"), None),
        P(("site", "structur"), None),
        P("scenario"),
        P("scenario", None),
    )
    out_specs = P(("scenario", "site", "structur"), None, None, None)
    return jax.shard_map(
        per_device, mesh=mesh, in_specs=in_specs, out_specs=out_specs, check_vma=False
    )
```

```python
import functools

import jax
import jax.numpy as jnp
from jax import lax
from jax.experimental import pallas as pl
from jax.experimental.pallas import tpu as pltpu
from jax.sharding import PartitionSpec as P

GRID_AXES = ("site", "structur", "sub")
ALL_AXES = ("scenario",) + GRID_AXES
SMEM = pl.BlockSpec(memory_space=pltpu.SMEM)
VMEM = pl.BlockSpec(memory_space=pltpu.VMEM)
ANY = pl.BlockSpec(memory_space=pl.ANY)
SMALL = pltpu.CompilerParams(vmem_limit_bytes=4 << 20)

SLOT, LATE, NEWS, ORDER, PLACE = range(5)
CHUNK = 4
PIECES = 4


def held(x):
    return pltpu.with_memory_space_constraint(x, pltpu.VMEM)


def far(x):
    return pltpu.with_memory_space_constraint(x, pltpu.HBM)


def table(x):
    return pltpu.with_memory_space_constraint(x, pltpu.SMEM)


def partner_site(site, kind, sites):
    other = site ^ 1 if kind == "even" else (site + 1 if site % 2 else site - 1)
    return other if 0 <= other < sites else None


def link_pairs(kind, turn, sites, groups):
    pairs = []
    for site in range(sites):
        to_site = site if kind == "own" else partner_site(site, kind, sites)
        if to_site is None:
            continue
        for member in range(groups):
            pairs.append(
                (site * groups + member, to_site * groups + (member - turn) % groups)
            )
    return pairs


def swap_cores(x):
    return lax.ppermute(x, "sub", [(0, 1), (1, 0)])


def planes_kernel(history, planes, sem):
    core = lax.axis_index("sub")
    count = planes.shape[0]
    copy = pltpu.make_async_copy(
        history.at[pl.ds(core * (count - 1), count)], planes, sem
    )
    copy.start()
    copy.wait()


def table_kernel(slots, sites, groups, *refs):
    src, delay, tiles, after = refs[:4]
    *taps, whole, meta, src_buf, delay_buf, sem = refs[4:]
    part = taps[0].shape[0]
    site, member, core = (lax.axis_index(a) for a in GRID_AXES)
    rows = tiles.shape[2]
    copies = [
        pltpu.make_async_copy(src, src_buf, sem.at[0]),
        pltpu.make_async_copy(delay, delay_buf, sem.at[1]),
    ] + [
        pltpu.make_async_copy(tiles.at[pl.ds(n * part, part), 0], out, sem.at[2 + n])
        for n, out in enumerate(taps)
    ]
    copies.append(pltpu.make_async_copy(tiles, whole, sem.at[2 + len(taps)]))
    for copy in copies:
        copy.start()
    copies[0].wait()
    copies[1].wait()
    even_step = jnp.where(site % 2 == 0, 1, -1)
    ahead = jnp.int32(0)
    behind = jnp.int32(src.shape[1])
    for p in range(src.shape[1]):
        value, wait = src_buf[0, p], delay_buf[0, p]
        turn = (value % groups - member + groups) % groups
        dist = value // groups - site
        kind = jnp.where(dist == 0, 2, jnp.where(dist == even_step, 1, 0))
        key = kind * groups + turn
        slot = jnp.int32(-1)
        for n in range(3 * groups):
            mine = jnp.where(core == 0, slots[0][n], slots[1][n])
            slot = jnp.where(key == n, mine, slot)
        mine = jnp.where(kind == 2, 0, jnp.where(kind == 1 - core, 1, -1))
        news = jnp.logical_and(wait == 1, mine >= 0)
        meta[SLOT, p] = slot
        meta[LATE, p] = wait - 1
        meta[NEWS, p] = jnp.where(news, 2 * turn + mine, -1)
        relayed = slot >= groups + 2
        behind = behind - jnp.where(relayed, 0, 1)
        meta[ORDER, jnp.where(relayed, ahead, behind)] = p
        ahead = ahead + jnp.where(relayed, 1, 0)
        meta[PLACE, p] = core
    meta[PLACE, 0] = (site * groups + member) * rows
    meta[PLACE, 2] = ahead
    for copy in copies[2:]:
        copy.wait()


def swapped_kernel(count, meta, tiles, acc, *refs):
    sources, pieces = refs[:count], refs[count:-3]
    extra, newest, total = refs[-3:]
    part = pieces[0].shape[0]
    taps = tiles.shape[1]
    width = sources[0].shape[2]
    core = meta[PLACE, 1]
    total[...] = acc[...]
    for n, piece in enumerate(pieces):
        extra[n * part : (n + 1) * part] = piece[...]

    @pl.when(core == 1)
    def _():
        newest[...] = extra[...]

    @pl.when(core == 0)
    def _():
        newest[...] = tiles[:, 0]

        @pl.loop(0, tiles.shape[0])
        def _(p):
            for slot, source in enumerate(sources):
                used = jnp.logical_and(meta[SLOT, p] == slot, meta[LATE, p] == 0)

                @pl.when(used)
                def _():
                    total[:, width:] += jnp.dot(
                        extra[p], source[taps - 1], preferred_element_type=jnp.float32
                    )


def swapped_part(meta, tiles, acc, sources, pieces):
    whole = pltpu.VMEM(tiles.shape[:1] + tiles.shape[2:], tiles.dtype)
    return pl.pallas_call(
        functools.partial(swapped_kernel, len(sources)),
        out_shape=[whole, whole, pltpu.VMEM(acc.shape, acc.dtype)],
        in_specs=[SMEM] + [VMEM] * (2 + len(sources) + len(pieces)),
        out_specs=[VMEM] * 3,
        compiler_params=SMALL,
        name="swapped_part",
    )(table(meta), held(tiles), held(acc), *[held(x) for x in sources + pieces])


def near_kernel(count, meta, tiles, *refs):
    sources, (total,) = refs[:count], refs[count:]
    taps = tiles.shape[1]
    total[...] = jnp.zeros_like(total)

    def one(p, source):
        late = meta[LATE, p]
        empty = jnp.zeros(source.shape[1:], source.dtype)
        right = jnp.where(late == 1, source[0], empty)
        planes = []
        for k in range(taps):
            planes.append(jnp.concatenate([source[late + k], right], axis=1))
            right = source[late + k]
        total[...] += jnp.dot(
            jnp.concatenate([tiles[p, k] for k in range(taps)], axis=1),
            jnp.concatenate(planes, axis=0),
            preferred_element_type=jnp.float32,
        )

    @pl.loop(0, tiles.shape[0])
    def _(p):
        for slot, source in enumerate(sources):
            pl.when(meta[SLOT, p] == slot)(functools.partial(one, p, source))


def near_part(meta, tiles, sources):
    rows, width = sources[0].shape[1:]
    return pl.pallas_call(
        functools.partial(near_kernel, len(sources)),
        out_shape=pltpu.VMEM((rows, 2 * width), jnp.float32),
        in_specs=[SMEM] + [VMEM] * (1 + len(sources)),
        out_specs=VMEM,
        compiler_params=SMALL,
        name="near_part",
    )(table(meta), held(tiles), *[held(x) for x in sources])


def relayed_kernel(first, count, meta, tiles, extra, acc, *refs):
    sources, (out0, out1, total, store) = refs[:count], refs[count:]
    planes, _, width = sources[0].shape
    pairs, taps = tiles.shape[:2]
    none = count * planes
    for n, source in enumerate(sources):
        store[n * planes : (n + 1) * planes] = source[...]
    store[none] = jnp.zeros(store.shape[1:], store.dtype)
    total[...] = acc[...]

    def chunk(start):
        numbers, left, right, swapped = [], [], [], []
        for i in range(start, start + CHUNK):
            p = meta[ORDER, i]
            used = i < meta[PLACE, 2]
            late = meta[LATE, p]
            base = (meta[SLOT, p] - first) * planes
            numbers.append(p)
            places = [jnp.where(used, base + late + k, none) for k in range(taps)]
            before = jnp.where(jnp.logical_and(used, late == 1), base, none)
            left += places
            right += [before] + places[:-1]
            swapped.append(
                jnp.where(jnp.logical_and(used, late == 0), base + taps - 1, none)
            )
        total[...] += jnp.dot(
            jnp.concatenate([tiles[p, k] for p in numbers for k in range(taps)], axis=1),
            jnp.concatenate(
                [
                    jnp.concatenate([store[a], store[b]], axis=1)
                    for a, b in zip(left, right)
                ],
                axis=0,
            ),
            preferred_element_type=jnp.float32,
        )

        @pl.when(meta[PLACE, 1] == 0)
        def _():
            total[:, width:] += jnp.dot(
                jnp.concatenate([extra[p] for p in numbers], axis=1),
                jnp.concatenate([store[a] for a in swapped], axis=0),
                preferred_element_type=jnp.float32,
            )

    for start in range(0, pairs, CHUNK):
        pl.when(meta[PLACE, 2] > start)(functools.partial(chunk, start))
    out0[...] = total[:, :width]
    out1[...] = total[:, width:]


def relayed_part(meta, tiles, extra, acc, sources, first):
    planes, rows, width = sources[0].shape
    store = (len(sources) * planes + 1, rows, width)
    half = pltpu.VMEM((rows, width), jnp.float32)
    room = 2 * store[0] * rows * width + 4 * acc.size
    return pl.pallas_call(
        functools.partial(relayed_kernel, first, len(sources)),
        out_shape=[half, half],
        in_specs=[SMEM] + [VMEM] * (3 + len(sources)),
        out_specs=[VMEM, VMEM],
        scratch_shapes=[
            pltpu.VMEM(acc.shape, acc.dtype),
            pltpu.VMEM(store, sources[0].dtype),
        ],
        compiler_params=pltpu.CompilerParams(vmem_limit_bytes=room + (4 << 20)),
        name="relayed_part",
    )(table(meta), held(tiles), held(extra), held(acc), *[held(x) for x in sources])


def solve_rows(base, mine, other, inverse, strike, wave):
    rows, width = mine.shape
    segments = base + lax.broadcasted_iota(jnp.int32, (rows, width), 0)
    incident = jnp.where(segments == strike, wave, jnp.float32(0.0))
    rhs = (incident - (mine + other)).astype(jnp.bfloat16)
    return jnp.dot(inverse, rhs, preferred_element_type=jnp.float32).astype(
        jnp.bfloat16
    )


def first_kernel(meta, mine, other, inverse, strike, wave, out):
    out[...] = solve_rows(
        meta[PLACE, 0], mine[...], other[...], inverse[...], strike[...], wave[0:1, :]
    )


def second_kernel(meta, first, mine, other, inverse, strike, wave, out):
    out[0] = first[...]
    out[1] = solve_rows(
        meta[PLACE, 0], mine[...], other[...], inverse[...], strike[...], wave[1:2, :]
    )


def pack_kernel(meta, own, other, out):
    half = own.shape[0] // 2

    @pl.when(meta[PLACE, 1] == 0)
    def _():
        out[:half] = own[:half]

    @pl.when(meta[PLACE, 1] == 1)
    def _():
        out[:half] = own[half:]

    out[half:] = other[...]


def pack(meta, own, other):
    rows, width = own.shape
    return pl.pallas_call(
        pack_kernel,
        out_shape=pltpu.VMEM((rows // 2 + rows, width), own.dtype),
        in_specs=[SMEM] + [VMEM] * 2,
        out_specs=VMEM,
        compiler_params=SMALL,
        name="pack",
    )(table(meta), held(own), held(other))


def fresh_kernel(turn, meta, tiles, source, acc, out):
    out[...] = acc[...]
    half = tiles.shape[2] // 2
    core = meta[PLACE, 1]

    def add(left, right):
        out[...] += jnp.dot(left, right, preferred_element_type=jnp.float32)

    @pl.loop(0, tiles.shape[0])
    def _(p):
        news = meta[NEWS, p]

        @pl.when(jnp.logical_and(news == 2 * turn, core == 0))
        def _():
            add(tiles[p, :, :half], source[:half])

        @pl.when(jnp.logical_and(news == 2 * turn, core == 1))
        def _():
            add(tiles[p, :, half:], source[:half])

        @pl.when(news == 2 * turn + 1)
        def _():
            add(tiles[p], source[half:])


def fresh_part(meta, tiles, source, turn, acc):
    return pl.pallas_call(
        functools.partial(fresh_kernel, turn),
        out_shape=pltpu.VMEM(acc.shape, acc.dtype),
        in_specs=[SMEM] + [VMEM] * 3,
        out_specs=VMEM,
        compiler_params=SMALL,
        name="fresh_part",
    )(table(meta), held(tiles), held(source), held(acc))


def per_device(tiles, history, self_inverse, pair_src, pair_delay, strike_seg, waveform):
    sites, groups = lax.axis_size("site"), lax.axis_size("structur")
    tiles, history, inverse = tiles[0], history[0], self_inverse[0]
    pairs, taps, rows, cols = tiles.shape
    width = history.shape[2]

    kinds = ("odd", "even", "own")
    key = {(k, t): n * groups + t for n, k in enumerate(kinds) for t in range(groups)}

    def send(x, *messages):
        scenarios, grid = lax.axis_size("scenario"), sites * groups * 2
        pairs = []
        for scenario in range(scenarios):
            twin = scenario ^ 1
            for c, m in enumerate(messages):
                moves = dict(link_pairs(*m, sites, groups))
                for a in range(sites * groups):
                    source = scenario * grid + 2 * a + c
                    if a in moves:
                        pairs.append((source, scenario * grid + 2 * moves[a] + c))
                    elif twin < scenarios:
                        pairs.append((source, twin * grid + 2 * a + c))
        return lax.ppermute(x, ALL_AXES, pairs)

    slots = [[-1] * (3 * groups) for _ in range(2)]
    for c in range(2):
        for t in range(groups):
            slots[c][key["own", t]] = t
            for n, kind in enumerate(("even", "odd")):
                slots[c][key[kind, t]] = groups + 2 * t + (n ^ c)

    planes = pl.pallas_call(
        planes_kernel,
        out_shape=pltpu.VMEM((taps + 1, rows, width), history.dtype),
        in_specs=[ANY],
        out_specs=VMEM,
        scratch_shapes=[pltpu.SemaphoreType.DMA],
        compiler_params=SMALL,
        name="own_planes",
    )(far(history))
    *taps0, tiles, meta = pl.pallas_call(
        functools.partial(table_kernel, slots, sites, groups),
        out_shape=[pltpu.VMEM((pairs // PIECES, rows, cols), tiles.dtype)] * PIECES
        + [pltpu.VMEM(tiles.shape, tiles.dtype), pltpu.SMEM((5, pairs), jnp.int32)],
        in_specs=[ANY] * 4,
        out_specs=[VMEM] * (PIECES + 1) + [SMEM],
        scratch_shapes=[
            pltpu.SMEM((1, pairs), jnp.int32),
            pltpu.SMEM((1, pairs), jnp.int32),
            pltpu.SemaphoreType.DMA((3 + PIECES,)),
        ],
        compiler_params=SMALL,
        name="table",
    )(far(pair_src), far(pair_delay), far(tiles), planes)

    own = [planes] + [send(planes, *[("own", t)] * 2) for t in range(1, groups)]
    partners = []
    for x in own:
        partners.append(send(x, ("even", 0), ("odd", 0)))
        partners.append(send(x, ("odd", 0), ("even", 0)))
    pieces = [swap_cores(x) for x in taps0]

    near = own + partners[:2]
    acc = near_part(meta, tiles, near)
    extra, newest, acc = swapped_part(meta, tiles, acc, near, pieces)
    mine0, mine1 = relayed_part(meta, tiles, extra, acc, partners[2:], groups + 2)

    strike, inverse, wave = held(strike_seg[None, :]), held(inverse), held(waveform)
    current0 = pl.pallas_call(
        first_kernel,
        out_shape=pltpu.VMEM((rows, width), jnp.bfloat16),
        in_specs=[SMEM] + [VMEM] * 5,
        out_specs=VMEM,
        compiler_params=SMALL,
        name="first_currents",
    )(table(meta), held(mine0), held(swap_cores(mine0)), inverse, strike, wave)

    packed = pack(meta, current0, send(current0, ("even", 0), ("odd", 0)))
    passed = [send(packed, *[("own", t)] * 2) for t in range(1, groups)]
    for turn, block in enumerate([packed] + passed):
        mine1 = fresh_part(meta, newest, block, turn, mine1)

    currents = pl.pallas_call(
        second_kernel,
        out_shape=jax.ShapeDtypeStruct((2, rows, width), jnp.bfloat16),
        in_specs=[SMEM] + [VMEM] * 6,
        out_specs=VMEM,
        compiler_params=SMALL,
        name="second_currents",
    )(
        table(meta),
        held(current0),
        held(mine1),
        held(swap_cores(mine1)),
        inverse,
        strike,
        wave,
    )
    return currents[None]


def solution(mesh):
    in_specs = (
        P(("site", "structur"), None, "sub", None, None),
        P(("scenario", "site", "structur"), None, None, None),
        P(("site", "structur"), None, None),
        P(("site", "structur"), None),
        P(("site", "structur"), None),
        P("scenario"),
        P("scenario", None),
    )
    out_specs = P(("scenario", "site", "structur"), None, None, None)
    return jax.shard_map(
        per_device, mesh=mesh, in_specs=in_specs, out_specs=out_specs, check_vma=False
    )
```

```python
import functools
import itertools

import jax
import jax.numpy as jnp
from jax import lax
from jax.experimental import pallas as pl
from jax.experimental.pallas import tpu as pltpu
from jax.sharding import PartitionSpec as P

GRID_AXES = ("site", "structur", "sub")
ALL_AXES = ("scenario",) + GRID_AXES
SMEM = pl.BlockSpec(memory_space=pltpu.SMEM)
VMEM = pl.BlockSpec(memory_space=pltpu.VMEM)
ANY = pl.BlockSpec(memory_space=pl.ANY)
SMALL = pltpu.CompilerParams(vmem_limit_bytes=4 << 20)

SLOT, LATE, NEWS, ORDER, PLACE = range(5)
CHUNK = 4
PIECES = 4
HALVES = 1


def held(x):
    return pltpu.with_memory_space_constraint(x, pltpu.VMEM)


def far(x):
    return pltpu.with_memory_space_constraint(x, pltpu.HBM)


def table(x):
    return pltpu.with_memory_space_constraint(x, pltpu.SMEM)


def partner_site(site, kind, sites):
    other = site ^ 1 if kind == "even" else (site + 1 if site % 2 else site - 1)
    return other if 0 <= other < sites else None


def link_pairs(kind, turn, sites, groups):
    pairs = []
    for site in range(sites):
        to_site = site if kind == "own" else partner_site(site, kind, sites)
        if to_site is None:
            continue
        for member in range(groups):
            pairs.append(
                (site * groups + member, to_site * groups + (member - turn) % groups)
            )
    return pairs


def swap_cores(x):
    return lax.ppermute(x, "sub", [(0, 1), (1, 0)])


def planes_kernel(history, planes, sem):
    core = lax.axis_index("sub")
    count = planes.shape[0]
    copy = pltpu.make_async_copy(
        history.at[pl.ds(core * (count - 1), count)], planes, sem
    )
    copy.start()
    copy.wait()


def table_kernel(slots, news, sites, groups, *refs):
    src, delay, tiles, after = refs[:4]
    *taps, whole, meta, src_buf, delay_buf, sem = refs[4:]
    part = taps[0].shape[0]
    site, member, core = (lax.axis_index(a) for a in GRID_AXES)
    rows = tiles.shape[2]
    copies = [
        pltpu.make_async_copy(src, src_buf, sem.at[0]),
        pltpu.make_async_copy(delay, delay_buf, sem.at[1]),
    ] + [
        pltpu.make_async_copy(tiles.at[pl.ds(n * part, part), 0], out, sem.at[2 + n])
        for n, out in enumerate(taps)
    ]
    copies.append(pltpu.make_async_copy(tiles, whole, sem.at[2 + len(taps)]))
    for copy in copies:
        copy.start()
    copies[0].wait()
    copies[1].wait()
    even_step = jnp.where(site % 2 == 0, 1, -1)
    ahead = jnp.int32(0)
    behind = jnp.int32(src.shape[1])
    for p in range(src.shape[1]):
        value, wait = src_buf[0, p], delay_buf[0, p]
        turn = (value % groups - member + groups) % groups
        dist = value // groups - site
        kind = jnp.where(dist == 0, 2, jnp.where(dist == even_step, 1, 0))
        key = kind * groups + turn
        slot, fresh = jnp.int32(-1), jnp.int32(-1)
        for n in range(3 * groups):
            mine = [jnp.where(core == 0, t[0][n], t[1][n]) for t in (slots, news)]
            slot = jnp.where(key == n, mine[0], slot)
            fresh = jnp.where(key == n, mine[1], fresh)
        meta[SLOT, p] = slot
        meta[LATE, p] = wait - 1
        meta[NEWS, p] = jnp.where(wait == 1, fresh, -1)
        relayed = slot >= groups + 2
        behind = behind - jnp.where(relayed, 0, 1)
        meta[ORDER, jnp.where(relayed, ahead, behind)] = p
        ahead = ahead + jnp.where(relayed, 1, 0)
        meta[PLACE, p] = core
    meta[PLACE, 0] = (site * groups + member) * rows
    meta[PLACE, 2] = ahead
    for copy in copies[2:]:
        copy.wait()


def swapped_kernel(count, meta, tiles, acc, *refs):
    sources, pieces = refs[:count], refs[count:-3]
    extra, newest, total = refs[-3:]
    part = pieces[0].shape[0]
    taps = tiles.shape[1]
    width = sources[0].shape[2]
    core = meta[PLACE, 1]
    total[...] = acc[...]
    for n, piece in enumerate(pieces):
        extra[n * part : (n + 1) * part] = piece[...]

    @pl.when(core == 1)
    def _():
        newest[...] = extra[...]

    @pl.when(core == 0)
    def _():
        newest[...] = tiles[:, 0]

        @pl.loop(0, tiles.shape[0])
        def _(p):
            for slot, source in enumerate(sources):
                used = jnp.logical_and(meta[SLOT, p] == slot, meta[LATE, p] == 0)

                @pl.when(used)
                def _():
                    total[:, width:] += jnp.dot(
                        extra[p], source[taps - 1], preferred_element_type=jnp.float32
                    )


def swapped_part(meta, tiles, acc, sources, pieces):
    whole = pltpu.VMEM(tiles.shape[:1] + tiles.shape[2:], tiles.dtype)
    return pl.pallas_call(
        functools.partial(swapped_kernel, len(sources)),
        out_shape=[whole, whole, pltpu.VMEM(acc.shape, acc.dtype)],
        in_specs=[SMEM] + [VMEM] * (2 + len(sources) + len(pieces)),
        out_specs=[VMEM] * 3,
        compiler_params=SMALL,
        name="swapped_part",
    )(table(meta), held(tiles), held(acc), *[held(x) for x in sources + pieces])


def row_pieces(rows, start, stop):
    for plane in range(start // rows, -(-stop // rows)):
        low, high = max(start, plane * rows), min(stop, (plane + 1) * rows)
        yield plane, low - plane * rows, high - plane * rows, low - start


def heads_kernel(head, *refs):
    sources, out = refs[:-1], refs[-1]
    for n, source in enumerate(sources):
        for plane, low, high, place in row_pieces(source.shape[1], 0, head):
            place += n * head
            out[place : place + high - low] = source[plane, low:high]


def heads(sources, head):
    width = sources[0].shape[2]
    return pl.pallas_call(
        functools.partial(heads_kernel, head),
        out_shape=pltpu.VMEM((len(sources) * head, width), sources[0].dtype),
        in_specs=[VMEM] * len(sources),
        out_specs=VMEM,
        compiler_params=SMALL,
        name="heads",
    )(*[held(x) for x in sources])


def tail_kernel(head, source, out):
    planes, rows, _ = source.shape
    for plane, low, high, place in row_pieces(rows, head, planes * rows):
        out[place : place + high - low] = source[plane, low:high]


def tail(source, head):
    planes, rows, width = source.shape
    return pl.pallas_call(
        functools.partial(tail_kernel, head),
        out_shape=pltpu.VMEM((planes * rows - head, width), source.dtype),
        in_specs=[VMEM],
        out_specs=VMEM,
        compiler_params=SMALL,
        name="tail",
    )(held(source))


def near_kernel(count, meta, tiles, *refs):
    sources, (total,) = refs[:count], refs[count:]
    taps = tiles.shape[1]
    total[...] = jnp.zeros_like(total)

    def one(p, source):
        late = meta[LATE, p]
        empty = jnp.zeros(source.shape[1:], source.dtype)
        right = jnp.where(late == 1, source[0], empty)
        planes = []
        for k in range(taps):
            planes.append(jnp.concatenate([source[late + k], right], axis=1))
            right = source[late + k]
        total[...] += jnp.dot(
            jnp.concatenate([tiles[p, k] for k in range(taps)], axis=1),
            jnp.concatenate(planes, axis=0),
            preferred_element_type=jnp.float32,
        )

    @pl.loop(0, tiles.shape[0])
    def _(p):
        for slot, source in enumerate(sources):
            pl.when(meta[SLOT, p] == slot)(functools.partial(one, p, source))


def near_part(meta, tiles, sources):
    rows, width = sources[0].shape[1:]
    return pl.pallas_call(
        functools.partial(near_kernel, len(sources)),
        out_shape=pltpu.VMEM((rows, 2 * width), jnp.float32),
        in_specs=[SMEM] + [VMEM] * (1 + len(sources)),
        out_specs=VMEM,
        compiler_params=SMALL,
        name="near_part",
    )(table(meta), held(tiles), *[held(x) for x in sources])


def relayed_kernel(first, turns, head, meta, tiles, extra, acc, *refs):
    sources, (out0, out1, total, store) = refs[: 3 * turns], refs[3 * turns :]
    pairs, taps, rows = tiles.shape[:3]
    planes, width = taps + 1, acc.shape[1] // 2
    none = 2 * turns * planes
    for turn in range(turns):
        tops, *rests = sources[3 * turn : 3 * turn + 3]
        for n, rest in enumerate(rests):
            base = (2 * turn + n) * planes
            for plane, low, high, place in row_pieces(rows, 0, head):
                place += n * head
                store[base + plane, low:high] = tops[place : place + high - low]
            for plane, low, high, place in row_pieces(rows, head, planes * rows):
                store[base + plane, low:high] = rest[place : place + high - low]
    store[none] = jnp.zeros(store.shape[1:], store.dtype)
    total[...] = acc[...]

    def chunk(start):
        numbers, left, right, swapped = [], [], [], []
        for i in range(start, start + CHUNK):
            p = meta[ORDER, i]
            used = i < meta[PLACE, 2]
            late = meta[LATE, p]
            base = (meta[SLOT, p] - first) * planes
            numbers.append(p)
            places = [jnp.where(used, base + late + k, none) for k in range(taps)]
            before = jnp.where(jnp.logical_and(used, late == 1), base, none)
            left += places
            right += [before] + places[:-1]
            swapped.append(
                jnp.where(jnp.logical_and(used, late == 0), base + taps - 1, none)
            )
        total[...] += jnp.dot(
            jnp.concatenate([tiles[p, k] for p in numbers for k in range(taps)], axis=1),
            jnp.concatenate(
                [
                    jnp.concatenate([store[a], store[b]], axis=1)
                    for a, b in zip(left, right)
                ],
                axis=0,
            ),
            preferred_element_type=jnp.float32,
        )

        @pl.when(meta[PLACE, 1] == 0)
        def _():
            total[:, width:] += jnp.dot(
                jnp.concatenate([extra[p] for p in numbers], axis=1),
                jnp.concatenate([store[a] for a in swapped], axis=0),
                preferred_element_type=jnp.float32,
            )

    for start in range(0, pairs, CHUNK):
        pl.when(meta[PLACE, 2] > start)(functools.partial(chunk, start))
    out0[...] = total[:, :width]
    out1[...] = total[:, width:]


def relayed_part(meta, tiles, extra, acc, sources, head, first):
    taps, rows = tiles.shape[1:3]
    width, turns = acc.shape[1] // 2, len(sources) // 3
    store = (2 * turns * (taps + 1) + 1, rows, width)
    half = pltpu.VMEM((rows, width), jnp.float32)
    room = 2 * store[0] * rows * width + 4 * acc.size
    return pl.pallas_call(
        functools.partial(relayed_kernel, first, turns, head),
        out_shape=[half, half],
        in_specs=[SMEM] + [VMEM] * (3 + len(sources)),
        out_specs=[VMEM, VMEM],
        scratch_shapes=[
            pltpu.VMEM(acc.shape, acc.dtype),
            pltpu.VMEM(store, sources[0].dtype),
        ],
        compiler_params=pltpu.CompilerParams(vmem_limit_bytes=room + (4 << 20)),
        name="relayed_part",
    )(table(meta), held(tiles), held(extra), held(acc), *[held(x) for x in sources])


def solve_rows(base, mine, other, inverse, strike, wave):
    rows, width = mine.shape
    segments = base + lax.broadcasted_iota(jnp.int32, (rows, width), 0)
    incident = jnp.where(segments == strike, wave, jnp.float32(0.0))
    rhs = (incident - (mine + other)).astype(jnp.bfloat16)
    return jnp.dot(inverse, rhs, preferred_element_type=jnp.float32).astype(
        jnp.bfloat16
    )


def first_kernel(meta, mine, other, inverse, strike, wave, out):
    out[...] = solve_rows(
        meta[PLACE, 0], mine[...], other[...], inverse[...], strike[...], wave[0:1, :]
    )


def second_kernel(meta, first, mine, other, inverse, strike, wave, out):
    out[0] = first[...]
    out[1] = solve_rows(
        meta[PLACE, 0], mine[...], other[...], inverse[...], strike[...], wave[1:2, :]
    )


def fresh_kernel(number, meta, tiles, source, acc, out):
    out[...] = acc[...]

    @pl.loop(0, tiles.shape[0])
    def _(p):
        @pl.when(meta[NEWS, p] == number)
        def _():
            out[...] += jnp.dot(
                tiles[p], source[...], preferred_element_type=jnp.float32
            )


def fresh_part(meta, tiles, source, number, acc):
    return pl.pallas_call(
        functools.partial(fresh_kernel, number),
        out_shape=pltpu.VMEM(acc.shape, acc.dtype),
        in_specs=[SMEM] + [VMEM] * 3,
        out_specs=VMEM,
        compiler_params=SMALL,
        name="fresh_part",
    )(table(meta), held(tiles), held(source), held(acc))


def per_device(tiles, history, self_inverse, pair_src, pair_delay, strike_seg, waveform):
    sites, groups = lax.axis_size("site"), lax.axis_size("structur")
    tiles, history, inverse = tiles[0], history[0], self_inverse[0]
    pairs, taps, rows, cols = tiles.shape
    width = history.shape[2]

    kinds = ("odd", "even", "own")
    key = {(k, t): n * groups + t for n, k in enumerate(kinds) for t in range(groups)}

    def send(x, *messages):
        scenarios, grid = lax.axis_size("scenario"), sites * groups * 2
        pairs = []
        for scenario in range(scenarios):
            twin = scenario ^ 1
            for c, m in enumerate(messages):
                moves = dict(link_pairs(*m, sites, groups)) if m else {}
                for a in range(sites * groups):
                    source = scenario * grid + 2 * a + c
                    if a in moves:
                        pairs.append((source, scenario * grid + 2 * moves[a] + c))
                    elif twin < scenarios:
                        pairs.append((source, twin * grid + 2 * a + c))
        return lax.ppermute(x, ALL_AXES, pairs)

    slots = [[-1] * (3 * groups) for _ in range(2)]
    for c in range(2):
        for t in range(groups):
            slots[c][key["own", t]] = t
            for n, kind in enumerate(("even", "odd")):
                slots[c][key[kind, t]] = groups + 2 * t + (n ^ c)

    straight = [("own", t) for t in range(1, groups)] + [("even", 0), ("odd", 0)]
    diagonal = [(kind, t) for t in range(1, groups) for kind in ("even", "odd")]
    while len(diagonal) > len(straight):
        straight.append(diagonal.pop())
    rounds = list(itertools.zip_longest(straight, diagonal))
    news = [[-1] * (3 * groups) for _ in range(2)]
    news[1][key["own", 0]] = 0
    for n, messages in enumerate(rounds):
        for c, m in enumerate(messages):
            if m is not None:
                news[c][key[m]] = 1 + n

    planes = pl.pallas_call(
        planes_kernel,
        out_shape=pltpu.VMEM((taps + 1, rows, width), history.dtype),
        in_specs=[ANY],
        out_specs=VMEM,
        scratch_shapes=[pltpu.SemaphoreType.DMA],
        compiler_params=SMALL,
        name="own_planes",
    )(far(history))
    *taps0, tiles, meta = pl.pallas_call(
        functools.partial(table_kernel, slots, news, sites, groups),
        out_shape=[pltpu.VMEM((pairs // PIECES, rows, cols), tiles.dtype)] * PIECES
        + [pltpu.VMEM(tiles.shape, tiles.dtype), pltpu.SMEM((5, pairs), jnp.int32)],
        in_specs=[ANY] * 4,
        out_specs=[VMEM] * (PIECES + 1) + [SMEM],
        scratch_shapes=[
            pltpu.SMEM((1, pairs), jnp.int32),
            pltpu.SMEM((1, pairs), jnp.int32),
            pltpu.SemaphoreType.DMA((3 + PIECES,)),
        ],
        compiler_params=SMALL,
        name="table",
    )(far(pair_src), far(pair_delay), far(tiles), planes)

    own = [planes] + [send(planes, *[("own", t)] * 2) for t in range(1, groups)]
    partners = [
        send(planes, ("even", 0), ("odd", 0)),
        send(planes, ("odd", 0), ("even", 0)),
    ]
    head = HALVES * rows // 2
    tops = heads(partners, head)
    relayed = []
    for t in range(1, groups):
        rest = tail(own[t], head)
        relayed += [
            send(tops, *[("own", t)] * 2),
            send(rest, ("even", 0), ("odd", 0)),
            send(rest, ("odd", 0), ("even", 0)),
        ]
    pieces = [swap_cores(x) for x in taps0]

    near = own + partners
    acc = near_part(meta, tiles, near)
    extra, newest, acc = swapped_part(meta, tiles, acc, near, pieces)
    mine0, mine1 = relayed_part(
        meta, tiles, extra, acc, relayed, head, groups + 2
    )

    strike, inverse, wave = held(strike_seg[None, :]), held(inverse), held(waveform)
    current0 = pl.pallas_call(
        first_kernel,
        out_shape=pltpu.VMEM((rows, width), jnp.bfloat16),
        in_specs=[SMEM] + [VMEM] * 5,
        out_specs=VMEM,
        compiler_params=SMALL,
        name="first_currents",
    )(table(meta), held(mine0), held(swap_cores(mine0)), inverse, strike, wave)

    fresh = [send(current0, *messages) for messages in rounds]
    for number, block in enumerate([current0] + fresh):
        mine1 = fresh_part(meta, newest, block, number, mine1)

    currents = pl.pallas_call(
        second_kernel,
        out_shape=jax.ShapeDtypeStruct((2, rows, width), jnp.bfloat16),
        in_specs=[SMEM] + [VMEM] * 6,
        out_specs=VMEM,
        compiler_params=SMALL,
        name="second_currents",
    )(
        table(meta),
        held(current0),
        held(mine1),
        held(swap_cores(mine1)),
        inverse,
        strike,
        wave,
    )
    return currents[None]


def solution(mesh):
    in_specs = (
        P(("site", "structur"), None, "sub", None, None),
        P(("scenario", "site", "structur"), None, None, None),
        P(("site", "structur"), None, None),
        P(("site", "structur"), None),
        P(("site", "structur"), None),
        P("scenario"),
        P("scenario", None),
    )
    out_specs = P(("scenario", "site", "structur"), None, None, None)
    return jax.shard_map(
        per_device, mesh=mesh, in_specs=in_specs, out_specs=out_specs, check_vma=False
    )
```

```python
import functools
import itertools

import jax
import jax.numpy as jnp
from jax import lax
from jax.experimental import pallas as pl
from jax.experimental.pallas import tpu as pltpu
from jax.sharding import PartitionSpec as P

GRID_AXES = ("site", "structur", "sub")
ALL_AXES = ("scenario",) + GRID_AXES
SMEM = pl.BlockSpec(memory_space=pltpu.SMEM)
VMEM = pl.BlockSpec(memory_space=pltpu.VMEM)
ANY = pl.BlockSpec(memory_space=pl.ANY)
SMALL = pltpu.CompilerParams(vmem_limit_bytes=4 << 20)

SLOT, LATE, NEWS, ORDER, PLACE = range(5)
CHUNK = 4
PIECES = 4


def held(x):
    return pltpu.with_memory_space_constraint(x, pltpu.VMEM)


def far(x):
    return pltpu.with_memory_space_constraint(x, pltpu.HBM)


def table(x):
    return pltpu.with_memory_space_constraint(x, pltpu.SMEM)


def partner_site(site, kind, sites):
    other = site ^ 1 if kind == "even" else (site + 1 if site % 2 else site - 1)
    return other if 0 <= other < sites else None


def link_pairs(kind, turn, sites, groups):
    pairs = []
    for site in range(sites):
        to_site = site if kind == "own" else partner_site(site, kind, sites)
        if to_site is None:
            continue
        for member in range(groups):
            pairs.append(
                (site * groups + member, to_site * groups + (member - turn) % groups)
            )
    return pairs


def swap_cores(x):
    return lax.ppermute(x, "sub", [(0, 1), (1, 0)])


def planes_kernel(history, planes, sem):
    core = lax.axis_index("sub")
    count, rows, _ = history.shape
    taps, half = count // 2, rows // 2
    copies = [
        pltpu.make_async_copy(
            history.at[core * taps + n], planes.at[pl.ds(n * rows, rows)], sem.at[n]
        )
        for n in range(taps)
    ]
    copies.append(
        pltpu.make_async_copy(
            history.at[count - 1, pl.ds(core * half, half)],
            planes.at[pl.ds(taps * rows, half)],
            sem.at[taps],
        )
    )
    for copy in copies:
        copy.start()
    for copy in copies:
        copy.wait()


def table_kernel(slots, news, sites, groups, *refs):
    src, delay, tiles, after = refs[:4]
    *ends, whole, meta, src_buf, delay_buf, sem = refs[4:]
    part = ends[0].shape[0]
    site, member, core = (lax.axis_index(a) for a in GRID_AXES)
    rows = tiles.shape[2]
    copies = [
        pltpu.make_async_copy(src, src_buf, sem.at[0]),
        pltpu.make_async_copy(delay, delay_buf, sem.at[1]),
        pltpu.make_async_copy(tiles, whole, sem.at[2]),
    ]
    for copy in copies:
        copy.start()
    copies[0].wait()
    copies[1].wait()
    last = tiles.shape[1] - 1
    for p in range(src.shape[1]):
        copies.append(
            pltpu.make_async_copy(
                tiles.at[p, jnp.where(delay_buf[0, p] == 1, 0, last)],
                ends[p // part].at[p % part],
                sem.at[3 + p],
            )
        )
        copies[-1].start()
    even_step = jnp.where(site % 2 == 0, 1, -1)
    ahead = jnp.int32(0)
    behind = jnp.int32(src.shape[1])
    for p in range(src.shape[1]):
        value, wait = src_buf[0, p], delay_buf[0, p]
        turn = (value % groups - member + groups) % groups
        dist = value // groups - site
        kind = jnp.where(dist == 0, 2, jnp.where(dist == even_step, 1, 0))
        key = kind * groups + turn
        slot, fresh = jnp.int32(-1), jnp.int32(-1)
        for n in range(3 * groups):
            mine = [jnp.where(core == 0, t[0][n], t[1][n]) for t in (slots, news)]
            slot = jnp.where(key == n, mine[0], slot)
            fresh = jnp.where(key == n, mine[1], fresh)
        meta[SLOT, p] = slot
        meta[LATE, p] = wait - 1
        meta[NEWS, p] = jnp.where(wait == 1, fresh, -1)
        relayed = slot >= groups + 2
        behind = behind - jnp.where(relayed, 0, 1)
        meta[ORDER, jnp.where(relayed, ahead, behind)] = p
        ahead = ahead + jnp.where(relayed, 1, 0)
        meta[PLACE, p] = core
    meta[PLACE, 0] = (site * groups + member) * rows
    meta[PLACE, 2] = ahead
    for copy in copies[2:]:
        copy.wait()


def swapped_kernel(count, meta, tiles, acc, *refs):
    sources, pieces = refs[:count], refs[count:-4]
    cross, halves, newest, total = refs[-4:]
    part = pieces[0].shape[0]
    taps, rows = tiles.shape[1:3]
    half = rows // 2
    core = meta[PLACE, 1]
    total[...] = acc[...]
    for n, piece in enumerate(pieces):
        cross[n * part : (n + 1) * part] = piece[...]

    @pl.when(core == 0)
    def _():
        newest[...] = tiles[:, 0]
        halves[...] = cross[:, :, :half]

    @pl.when(core == 1)
    def _():
        newest[...] = cross[...]
        halves[...] = tiles[:, taps - 1, :, half:]

    @pl.loop(0, tiles.shape[0])
    def _(p):
        for slot, source in enumerate(sources):
            used, late = meta[SLOT, p] == slot, meta[LATE, p]
            width = source.shape[1]

            @pl.when(used & (late == 0) & (core == 0))
            def _():
                total[:, width:] += jnp.dot(
                    cross[p],
                    source[(taps - 1) * rows : taps * rows],
                    preferred_element_type=jnp.float32,
                )

            @pl.when(used & (late == 1))
            def _():
                total[:, :width] += jnp.dot(
                    halves[p],
                    source[taps * rows :],
                    preferred_element_type=jnp.float32,
                )

            @pl.when(used & (late == 1) & (core == 1))
            def _():
                total[:, :width] += jnp.dot(
                    cross[p], source[:rows], preferred_element_type=jnp.float32
                )


def swapped_part(meta, tiles, acc, sources, pieces):
    pairs, _, rows, cols = tiles.shape
    whole = pltpu.VMEM((pairs, rows, cols), tiles.dtype)
    return pl.pallas_call(
        functools.partial(swapped_kernel, len(sources)),
        out_shape=[
            whole,
            pltpu.VMEM((pairs, rows, cols // 2), tiles.dtype),
            whole,
            pltpu.VMEM(acc.shape, acc.dtype),
        ],
        in_specs=[SMEM] + [VMEM] * (2 + len(sources) + len(pieces)),
        out_specs=[VMEM] * 4,
        compiler_params=SMALL,
        name="swapped_part",
    )(table(meta), held(tiles), held(acc), *[held(x) for x in sources + pieces])


def near_kernel(count, meta, tiles, *refs):
    sources, (total,) = refs[:count], refs[count:]
    taps, rows = tiles.shape[1:3]
    total[...] = jnp.zeros_like(total)

    def one(p, source):
        late = meta[LATE, p]
        planes = [source[k * rows : (k + 1) * rows] for k in range(taps)]
        empty = jnp.zeros_like(planes[0])
        planes = [empty] + planes + [empty]
        both = [
            jnp.concatenate(
                [
                    jnp.where(late == 1, planes[k + 2], planes[k + 1]),
                    jnp.where(late == 1, planes[k + 1], planes[k]),
                ],
                axis=1,
            )
            for k in range(taps)
        ]
        total[...] += jnp.dot(
            jnp.concatenate([tiles[p, k] for k in range(taps)], axis=1),
            jnp.concatenate(both, axis=0),
            preferred_element_type=jnp.float32,
        )

    @pl.loop(0, tiles.shape[0])
    def _(p):
        for slot, source in enumerate(sources):
            pl.when(meta[SLOT, p] == slot)(functools.partial(one, p, source))


def near_part(meta, tiles, sources):
    rows, width = tiles.shape[2], sources[0].shape[1]
    return pl.pallas_call(
        functools.partial(near_kernel, len(sources)),
        out_shape=pltpu.VMEM((rows, 2 * width), jnp.float32),
        in_specs=[SMEM] + [VMEM] * (1 + len(sources)),
        out_specs=VMEM,
        compiler_params=SMALL,
        name="near_part",
    )(table(meta), held(tiles), *[held(x) for x in sources])


def relayed_kernel(first, count, meta, tiles, cross, halves, acc, *refs):
    sources, (out0, out1, total, store) = refs[:count], refs[count:]
    pairs, taps, rows = tiles.shape[:3]
    half, width = rows // 2, acc.shape[1] // 2
    block = taps * rows + half
    none = count * block
    core = meta[PLACE, 1]
    for n, source in enumerate(sources):
        store[n * block : (n + 1) * block] = source[...]
    store[none:] = jnp.zeros((rows, width), store.dtype)
    total[...] = acc[...]

    def plane(at, count):
        return store[pl.ds(pl.multiple_of(at, half), count)]

    def pair(a, b, count):
        return jnp.concatenate([plane(a, count), plane(b, count)], axis=1)

    def chunk(start):
        lefts, rights = [], []
        for i in range(start, start + CHUNK):
            p = meta[ORDER, i]
            used = i < meta[PLACE, 2]
            late = meta[LATE, p]
            base = (meta[SLOT, p] - first) * block
            early = jnp.logical_and(used, late == 0)
            after = jnp.logical_and(used, late == 1)
            ats = [jnp.where(used, base + k * rows, none) for k in range(taps)]
            before = [none] + ats + [none]
            for k in range(taps):
                lefts.append(tiles[p, k])
                a = jnp.where(late == 1, before[k + 2], before[k + 1])
                b = jnp.where(late == 1, before[k + 1], before[k])
                rights.append(pair(a, b, rows))
            lefts.append(cross[p])
            a = jnp.where(jnp.logical_and(after, core == 1), base, none)
            b = jnp.where(
                jnp.logical_and(early, core == 0), base + (taps - 1) * rows, none
            )
            rights.append(pair(a, b, rows))
            lefts.append(halves[p])
            a = jnp.where(after, base + taps * rows, none)
            rights.append(pair(a, none, half))
        total[...] += jnp.dot(
            jnp.concatenate(lefts, axis=1),
            jnp.concatenate(rights, axis=0),
            preferred_element_type=jnp.float32,
        )

    for start in range(0, pairs, CHUNK):
        pl.when(meta[PLACE, 2] > start)(functools.partial(chunk, start))
    out0[...] = total[:, :width]
    out1[...] = total[:, width:]


def relayed_part(meta, tiles, cross, halves, acc, sources, first):
    taps, rows = tiles.shape[1:3]
    width, count = acc.shape[1] // 2, len(sources)
    store = (count * (taps * rows + rows // 2) + rows, width)
    half = pltpu.VMEM((rows, width), jnp.float32)
    room = 2 * store[0] * width + 4 * acc.size
    return pl.pallas_call(
        functools.partial(relayed_kernel, first, count),
        out_shape=[half, half],
        in_specs=[SMEM] + [VMEM] * (4 + len(sources)),
        out_specs=[VMEM, VMEM],
        scratch_shapes=[
            pltpu.VMEM(acc.shape, acc.dtype),
            pltpu.VMEM(store, sources[0].dtype),
        ],
        compiler_params=pltpu.CompilerParams(vmem_limit_bytes=room + (4 << 20)),
        name="relayed_part",
    )(
        table(meta),
        held(tiles),
        held(cross),
        held(halves),
        held(acc),
        *[held(x) for x in sources],
    )


def solve_rows(base, mine, other, inverse, strike, wave):
    rows, width = mine.shape
    segments = base + lax.broadcasted_iota(jnp.int32, (rows, width), 0)
    incident = jnp.where(segments == strike, wave, jnp.float32(0.0))
    rhs = (incident - (mine + other)).astype(jnp.bfloat16)
    return jnp.dot(inverse, rhs, preferred_element_type=jnp.float32).astype(
        jnp.bfloat16
    )


def first_kernel(meta, mine, other, inverse, strike, wave, out):
    out[...] = solve_rows(
        meta[PLACE, 0], mine[...], other[...], inverse[...], strike[...], wave[0:1, :]
    )


def second_kernel(meta, first, mine, other, inverse, strike, wave, out):
    out[0] = first[...]
    out[1] = solve_rows(
        meta[PLACE, 0], mine[...], other[...], inverse[...], strike[...], wave[1:2, :]
    )


def fresh_kernel(number, meta, tiles, source, acc, out):
    out[...] = acc[...]

    @pl.loop(0, tiles.shape[0])
    def _(p):
        @pl.when(meta[NEWS, p] == number)
        def _():
            out[...] += jnp.dot(
                tiles[p], source[...], preferred_element_type=jnp.float32
            )


def fresh_part(meta, tiles, source, number, acc):
    return pl.pallas_call(
        functools.partial(fresh_kernel, number),
        out_shape=pltpu.VMEM(acc.shape, acc.dtype),
        in_specs=[SMEM] + [VMEM] * 3,
        out_specs=VMEM,
        compiler_params=SMALL,
        name="fresh_part",
    )(table(meta), held(tiles), held(source), held(acc))


def per_device(tiles, history, self_inverse, pair_src, pair_delay, strike_seg, waveform):
    sites, groups = lax.axis_size("site"), lax.axis_size("structur")
    tiles, history, inverse = tiles[0], history[0], self_inverse[0]
    pairs, taps, rows, cols = tiles.shape
    width = history.shape[2]

    kinds = ("odd", "even", "own")
    key = {(k, t): n * groups + t for n, k in enumerate(kinds) for t in range(groups)}

    def send(x, *messages):
        scenarios, grid = lax.axis_size("scenario"), sites * groups * 2
        pairs = []
        for scenario in range(scenarios):
            twin = scenario ^ 1
            for c, m in enumerate(messages):
                moves = dict(link_pairs(*m, sites, groups)) if m else {}
                for a in range(sites * groups):
                    source = scenario * grid + 2 * a + c
                    if a in moves:
                        pairs.append((source, scenario * grid + 2 * moves[a] + c))
                    elif twin < scenarios:
                        pairs.append((source, twin * grid + 2 * a + c))
        return lax.ppermute(x, ALL_AXES, pairs)

    slots = [[-1] * (3 * groups) for _ in range(2)]
    for c in range(2):
        for t in range(groups):
            slots[c][key["own", t]] = t
            for n, kind in enumerate(("even", "odd")):
                slots[c][key[kind, t]] = groups + 2 * t + (n ^ c)

    straight = [("own", t) for t in range(1, groups)] + [("even", 0), ("odd", 0)]
    diagonal = [(kind, t) for t in range(1, groups) for kind in ("even", "odd")]
    while len(diagonal) > len(straight):
        straight.append(diagonal.pop())
    rounds = list(itertools.zip_longest(straight, diagonal))
    news = [[-1] * (3 * groups) for _ in range(2)]
    news[1][key["own", 0]] = 0
    for n, messages in enumerate(rounds):
        for c, m in enumerate(messages):
            if m is not None:
                news[c][key[m]] = 1 + n

    planes = pl.pallas_call(
        planes_kernel,
        out_shape=pltpu.VMEM((taps * rows + rows // 2, width), history.dtype),
        in_specs=[ANY],
        out_specs=VMEM,
        scratch_shapes=[pltpu.SemaphoreType.DMA((taps + 1,))],
        compiler_params=SMALL,
        name="own_planes",
    )(far(history))
    *ends, tiles, meta = pl.pallas_call(
        functools.partial(table_kernel, slots, news, sites, groups),
        out_shape=[pltpu.VMEM((pairs // PIECES, rows, cols), tiles.dtype)] * PIECES
        + [pltpu.VMEM(tiles.shape, tiles.dtype), pltpu.SMEM((5, pairs), jnp.int32)],
        in_specs=[ANY] * 4,
        out_specs=[VMEM] * (PIECES + 1) + [SMEM],
        scratch_shapes=[
            pltpu.SMEM((1, pairs), jnp.int32),
            pltpu.SMEM((1, pairs), jnp.int32),
            pltpu.SemaphoreType.DMA((3 + pairs,)),
        ],
        compiler_params=SMALL,
        name="table",
    )(far(pair_src), far(pair_delay), far(tiles), planes)

    own = [planes] + [send(planes, *[("own", t)] * 2) for t in range(1, groups)]
    partners = [
        send(planes, ("even", 0), ("odd", 0)),
        send(planes, ("odd", 0), ("even", 0)),
    ]
    relayed = []
    for x in own[1:]:
        relayed.append(send(x, ("even", 0), ("odd", 0)))
        relayed.append(send(x, ("odd", 0), ("even", 0)))
    pieces = [swap_cores(x) for x in ends]

    near = own + partners
    acc = near_part(meta, tiles, near)
    cross, halves, newest, acc = swapped_part(meta, tiles, acc, near, pieces)
    mine0, mine1 = relayed_part(
        meta, tiles, cross, halves, acc, relayed, groups + 2
    )

    strike, inverse, wave = held(strike_seg[None, :]), held(inverse), held(waveform)
    current0 = pl.pallas_call(
        first_kernel,
        out_shape=pltpu.VMEM((rows, width), jnp.bfloat16),
        in_specs=[SMEM] + [VMEM] * 5,
        out_specs=VMEM,
        compiler_params=SMALL,
        name="first_currents",
    )(table(meta), held(mine0), held(swap_cores(mine0)), inverse, strike, wave)

    fresh = [send(current0, *messages) for messages in rounds]
    for number, block in enumerate([current0] + fresh):
        mine1 = fresh_part(meta, newest, block, number, mine1)

    currents = pl.pallas_call(
        second_kernel,
        out_shape=jax.ShapeDtypeStruct((2, rows, width), jnp.bfloat16),
        in_specs=[SMEM] + [VMEM] * 6,
        out_specs=VMEM,
        compiler_params=SMALL,
        name="second_currents",
    )(
        table(meta),
        held(current0),
        held(mine1),
        held(swap_cores(mine1)),
        inverse,
        strike,
        wave,
    )
    return currents[None]


def solution(mesh):
    in_specs = (
        P(("site", "structur"), None, "sub", None, None),
        P(("scenario", "site", "structur"), None, None, None),
        P(("site", "structur"), None, None),
        P(("site", "structur"), None),
        P(("site", "structur"), None),
        P("scenario"),
        P("scenario", None),
    )
    out_specs = P(("scenario", "site", "structur"), None, None, None)
    return jax.shard_map(
        per_device, mesh=mesh, in_specs=in_specs, out_specs=out_specs, check_vma=False
    )
```

```python
import functools
import itertools

import jax
import jax.numpy as jnp
from jax import lax
from jax.experimental import pallas as pl
from jax.experimental.pallas import tpu as pltpu
from jax.sharding import PartitionSpec as P

GRID_AXES = ("site", "structur", "sub")
ALL_AXES = ("scenario",) + GRID_AXES
SMEM = pl.BlockSpec(memory_space=pltpu.SMEM)
VMEM = pl.BlockSpec(memory_space=pltpu.VMEM)
ANY = pl.BlockSpec(memory_space=pl.ANY)
SMALL = pltpu.CompilerParams(vmem_limit_bytes=4 << 20)

SLOT, LATE, NEWS, ORDER, PLACE = range(5)
CHUNK = 4
PIECES = 4
HEAD = 96


def held(x):
    return pltpu.with_memory_space_constraint(x, pltpu.VMEM)


def far(x):
    return pltpu.with_memory_space_constraint(x, pltpu.HBM)


def table(x):
    return pltpu.with_memory_space_constraint(x, pltpu.SMEM)


def partner_site(site, kind, sites):
    other = site ^ 1 if kind == "even" else (site + 1 if site % 2 else site - 1)
    return other if 0 <= other < sites else None


def link_pairs(kind, turn, sites, groups):
    pairs = []
    for site in range(sites):
        to_site = site if kind == "own" else partner_site(site, kind, sites)
        if to_site is None:
            continue
        for member in range(groups):
            pairs.append(
                (site * groups + member, to_site * groups + (member - turn) % groups)
            )
    return pairs


def swap_cores(x):
    return lax.ppermute(x, "sub", [(0, 1), (1, 0)])


def planes_kernel(history, planes, sem):
    core = lax.axis_index("sub")
    count, rows, _ = history.shape
    taps, half = count // 2, rows // 2
    copies = [
        pltpu.make_async_copy(
            history.at[core * taps + n], planes.at[pl.ds(n * rows, rows)], sem.at[n]
        )
        for n in range(taps)
    ]
    copies.append(
        pltpu.make_async_copy(
            history.at[count - 1, pl.ds(core * half, half)],
            planes.at[pl.ds(taps * rows, half)],
            sem.at[taps],
        )
    )
    for copy in copies:
        copy.start()
    for copy in copies:
        copy.wait()


def table_kernel(slots, news, sites, groups, *refs):
    src, delay, tiles, after = refs[:4]
    *ends, whole, meta, src_buf, delay_buf, sem = refs[4:]
    part = ends[0].shape[0]
    site, member, core = (lax.axis_index(a) for a in GRID_AXES)
    rows = tiles.shape[2]
    copies = [
        pltpu.make_async_copy(src, src_buf, sem.at[0]),
        pltpu.make_async_copy(delay, delay_buf, sem.at[1]),
        pltpu.make_async_copy(tiles, whole, sem.at[2]),
    ]
    for copy in copies:
        copy.start()
    copies[0].wait()
    copies[1].wait()
    last = tiles.shape[1] - 1
    for p in range(src.shape[1]):
        copies.append(
            pltpu.make_async_copy(
                tiles.at[p, jnp.where(delay_buf[0, p] == 1, 0, last)],
                ends[p // part].at[p % part],
                sem.at[3 + p],
            )
        )
        copies[-1].start()
    even_step = jnp.where(site % 2 == 0, 1, -1)
    ahead = jnp.int32(0)
    behind = jnp.int32(src.shape[1])
    for p in range(src.shape[1]):
        value, wait = src_buf[0, p], delay_buf[0, p]
        turn = (value % groups - member + groups) % groups
        dist = value // groups - site
        kind = jnp.where(dist == 0, 2, jnp.where(dist == even_step, 1, 0))
        key = kind * groups + turn
        slot, fresh = jnp.int32(-1), jnp.int32(-1)
        for n in range(3 * groups):
            mine = [jnp.where(core == 0, t[0][n], t[1][n]) for t in (slots, news)]
            slot = jnp.where(key == n, mine[0], slot)
            fresh = jnp.where(key == n, mine[1], fresh)
        meta[SLOT, p] = slot
        meta[LATE, p] = wait - 1
        meta[NEWS, p] = jnp.where(wait == 1, fresh, -1)
        relayed = slot >= groups + 2
        behind = behind - jnp.where(relayed, 0, 1)
        meta[ORDER, jnp.where(relayed, ahead, behind)] = p
        ahead = ahead + jnp.where(relayed, 1, 0)
        meta[PLACE, p] = core
    meta[PLACE, 0] = (site * groups + member) * rows
    meta[PLACE, 2] = ahead
    for copy in copies[2:]:
        copy.wait()


def swapped_kernel(count, meta, tiles, acc, *refs):
    sources, pieces = refs[:count], refs[count:-4]
    cross, halves, newest, total = refs[-4:]
    part = pieces[0].shape[0]
    taps, rows = tiles.shape[1:3]
    half = rows // 2
    core = meta[PLACE, 1]
    total[...] = acc[...]
    for n, piece in enumerate(pieces):
        cross[n * part : (n + 1) * part] = piece[...]

    @pl.when(core == 0)
    def _():
        newest[...] = tiles[:, 0]
        halves[...] = cross[:, :, :half]

    @pl.when(core == 1)
    def _():
        newest[...] = cross[...]
        halves[...] = tiles[:, taps - 1, :, half:]

    @pl.loop(0, tiles.shape[0])
    def _(p):
        for slot, source in enumerate(sources):
            used, late = meta[SLOT, p] == slot, meta[LATE, p]
            width = source.shape[1]

            @pl.when(used & (late == 0) & (core == 0))
            def _():
                total[:, width:] += jnp.dot(
                    cross[p],
                    source[(taps - 1) * rows : taps * rows],
                    preferred_element_type=jnp.float32,
                )

            @pl.when(used & (late == 1))
            def _():
                total[:, :width] += jnp.dot(
                    halves[p],
                    source[taps * rows :],
                    preferred_element_type=jnp.float32,
                )

            @pl.when(used & (late == 1) & (core == 1))
            def _():
                total[:, :width] += jnp.dot(
                    cross[p], source[:rows], preferred_element_type=jnp.float32
                )


def swapped_part(meta, tiles, acc, sources, pieces):
    pairs, _, rows, cols = tiles.shape
    whole = pltpu.VMEM((pairs, rows, cols), tiles.dtype)
    return pl.pallas_call(
        functools.partial(swapped_kernel, len(sources)),
        out_shape=[
            whole,
            pltpu.VMEM((pairs, rows, cols // 2), tiles.dtype),
            whole,
            pltpu.VMEM(acc.shape, acc.dtype),
        ],
        in_specs=[SMEM] + [VMEM] * (2 + len(sources) + len(pieces)),
        out_specs=[VMEM] * 4,
        compiler_params=SMALL,
        name="swapped_part",
    )(table(meta), held(tiles), held(acc), *[held(x) for x in sources + pieces])


def cut_kernel(start, count, *refs):
    sources, out = refs[:-1], refs[-1]
    for n, source in enumerate(sources):
        out[n * count : (n + 1) * count] = source[start : start + count]


def cut(sources, start, count):
    width = sources[0].shape[1]
    return pl.pallas_call(
        functools.partial(cut_kernel, start, count),
        out_shape=pltpu.VMEM((len(sources) * count, width), sources[0].dtype),
        in_specs=[VMEM] * len(sources),
        out_specs=VMEM,
        compiler_params=SMALL,
        name="cut",
    )(*[held(x) for x in sources])


def near_kernel(count, meta, tiles, *refs):
    sources, (total,) = refs[:count], refs[count:]
    taps, rows = tiles.shape[1:3]
    total[...] = jnp.zeros_like(total)

    def one(p, source):
        late = meta[LATE, p]
        planes = [source[k * rows : (k + 1) * rows] for k in range(taps)]
        empty = jnp.zeros_like(planes[0])
        planes = [empty] + planes + [empty]
        both = [
            jnp.concatenate(
                [
                    jnp.where(late == 1, planes[k + 2], planes[k + 1]),
                    jnp.where(late == 1, planes[k + 1], planes[k]),
                ],
                axis=1,
            )
            for k in range(taps)
        ]
        total[...] += jnp.dot(
            jnp.concatenate([tiles[p, k] for k in range(taps)], axis=1),
            jnp.concatenate(both, axis=0),
            preferred_element_type=jnp.float32,
        )

    @pl.loop(0, tiles.shape[0])
    def _(p):
        for slot, source in enumerate(sources):
            pl.when(meta[SLOT, p] == slot)(functools.partial(one, p, source))


def near_part(meta, tiles, sources):
    rows, width = tiles.shape[2], sources[0].shape[1]
    return pl.pallas_call(
        functools.partial(near_kernel, len(sources)),
        out_shape=pltpu.VMEM((rows, 2 * width), jnp.float32),
        in_specs=[SMEM] + [VMEM] * (1 + len(sources)),
        out_specs=VMEM,
        compiler_params=SMALL,
        name="near_part",
    )(table(meta), held(tiles), *[held(x) for x in sources])


def relayed_kernel(first, turns, meta, tiles, cross, halves, acc, *refs):
    sources, (out0, out1, total, store) = refs[: 3 * turns], refs[3 * turns :]
    pairs, taps, rows = tiles.shape[:3]
    half, width = rows // 2, acc.shape[1] // 2
    block = taps * rows + half
    none = 2 * turns * block
    core = meta[PLACE, 1]
    for turn in range(turns):
        tops, *rests = sources[3 * turn : 3 * turn + 3]
        for n, rest in enumerate(rests):
            base = (2 * turn + n) * block
            store[base : base + HEAD] = tops[n * HEAD : (n + 1) * HEAD]
            store[base + HEAD : base + block] = rest[...]
    store[none:] = jnp.zeros((rows, width), store.dtype)
    total[...] = acc[...]

    def plane(at, count):
        return store[pl.ds(pl.multiple_of(at, half), count)]

    def pair(a, b, count):
        return jnp.concatenate([plane(a, count), plane(b, count)], axis=1)

    def chunk(start):
        lefts, rights = [], []
        for i in range(start, start + CHUNK):
            p = meta[ORDER, i]
            used = i < meta[PLACE, 2]
            late = meta[LATE, p]
            base = (meta[SLOT, p] - first) * block
            early = jnp.logical_and(used, late == 0)
            after = jnp.logical_and(used, late == 1)
            ats = [jnp.where(used, base + k * rows, none) for k in range(taps)]
            before = [none] + ats + [none]
            for k in range(taps):
                lefts.append(tiles[p, k])
                a = jnp.where(late == 1, before[k + 2], before[k + 1])
                b = jnp.where(late == 1, before[k + 1], before[k])
                rights.append(pair(a, b, rows))
            lefts.append(cross[p])
            a = jnp.where(jnp.logical_and(after, core == 1), base, none)
            b = jnp.where(
                jnp.logical_and(early, core == 0), base + (taps - 1) * rows, none
            )
            rights.append(pair(a, b, rows))
            lefts.append(halves[p])
            a = jnp.where(after, base + taps * rows, none)
            rights.append(pair(a, none, half))
        total[...] += jnp.dot(
            jnp.concatenate(lefts, axis=1),
            jnp.concatenate(rights, axis=0),
            preferred_element_type=jnp.float32,
        )

    for start in range(0, pairs, CHUNK):
        pl.when(meta[PLACE, 2] > start)(functools.partial(chunk, start))
    out0[...] = total[:, :width]
    out1[...] = total[:, width:]


def relayed_part(meta, tiles, cross, halves, acc, sources, first):
    taps, rows = tiles.shape[1:3]
    width, turns = acc.shape[1] // 2, len(sources) // 3
    store = (2 * turns * (taps * rows + rows // 2) + rows, width)
    half = pltpu.VMEM((rows, width), jnp.float32)
    room = 2 * store[0] * width + 4 * acc.size
    return pl.pallas_call(
        functools.partial(relayed_kernel, first, turns),
        out_shape=[half, half],
        in_specs=[SMEM] + [VMEM] * (4 + len(sources)),
        out_specs=[VMEM, VMEM],
        scratch_shapes=[
            pltpu.VMEM(acc.shape, acc.dtype),
            pltpu.VMEM(store, sources[0].dtype),
        ],
        compiler_params=pltpu.CompilerParams(vmem_limit_bytes=room + (4 << 20)),
        name="relayed_part",
    )(
        table(meta),
        held(tiles),
        held(cross),
        held(halves),
        held(acc),
        *[held(x) for x in sources],
    )


def solve_rows(base, mine, other, inverse, strike, wave):
    rows, width = mine.shape
    segments = base + lax.broadcasted_iota(jnp.int32, (rows, width), 0)
    incident = jnp.where(segments == strike, wave, jnp.float32(0.0))
    rhs = (incident - (mine + other)).astype(jnp.bfloat16)
    return jnp.dot(inverse, rhs, preferred_element_type=jnp.float32).astype(
        jnp.bfloat16
    )


def first_kernel(meta, mine, other, inverse, strike, wave, out):
    out[...] = solve_rows(
        meta[PLACE, 0], mine[...], other[...], inverse[...], strike[...], wave[0:1, :]
    )


def second_kernel(meta, first, mine, other, inverse, strike, wave, out):
    out[0] = first[...]
    out[1] = solve_rows(
        meta[PLACE, 0], mine[...], other[...], inverse[...], strike[...], wave[1:2, :]
    )


def fresh_kernel(number, meta, tiles, source, acc, out):
    out[...] = acc[...]

    @pl.loop(0, tiles.shape[0])
    def _(p):
        @pl.when(meta[NEWS, p] == number)
        def _():
            out[...] += jnp.dot(
                tiles[p], source[...], preferred_element_type=jnp.float32
            )


def fresh_part(meta, tiles, source, number, acc):
    return pl.pallas_call(
        functools.partial(fresh_kernel, number),
        out_shape=pltpu.VMEM(acc.shape, acc.dtype),
        in_specs=[SMEM] + [VMEM] * 3,
        out_specs=VMEM,
        compiler_params=SMALL,
        name="fresh_part",
    )(table(meta), held(tiles), held(source), held(acc))


def per_device(tiles, history, self_inverse, pair_src, pair_delay, strike_seg, waveform):
    sites, groups = lax.axis_size("site"), lax.axis_size("structur")
    tiles, history, inverse = tiles[0], history[0], self_inverse[0]
    pairs, taps, rows, cols = tiles.shape
    width = history.shape[2]

    kinds = ("odd", "even", "own")
    key = {(k, t): n * groups + t for n, k in enumerate(kinds) for t in range(groups)}

    def send(x, *messages):
        scenarios, grid = lax.axis_size("scenario"), sites * groups * 2
        pairs = []
        for scenario in range(scenarios):
            twin = scenario ^ 1
            for c, m in enumerate(messages):
                moves = dict(link_pairs(*m, sites, groups)) if m else {}
                for a in range(sites * groups):
                    source = scenario * grid + 2 * a + c
                    if a in moves:
                        pairs.append((source, scenario * grid + 2 * moves[a] + c))
                    elif twin < scenarios:
                        pairs.append((source, twin * grid + 2 * a + c))
        return lax.ppermute(x, ALL_AXES, pairs)

    swaps = ((("even", "odd"), ("odd", "even")), (("even", "odd"), ("odd", "even")))
    slots = [[-1] * (3 * groups) for _ in range(2)]
    for c in range(2):
        for t in range(groups):
            slots[c][key["own", t]] = t
            for n, pair in enumerate(swaps[min(t, 1)]):
                slots[c][key[pair[c], t]] = groups + 2 * t + n

    straight = [("odd", 0)]+[("own", t) for t in range(1, groups)]+[("even", 0)]
    diagonal = [(kind, t) for t in range(1, groups) for kind in ("even", "odd")]
    while len(diagonal) > len(straight):
        straight.append(diagonal.pop())
    rounds = list(itertools.zip_longest(straight, diagonal))
    news = [[-1] * (3 * groups) for _ in range(2)]
    news[1][key["own", 0]] = 0
    for n, messages in enumerate(rounds):
        for c, m in enumerate(messages):
            if m is not None:
                news[c][key[m]] = 1 + n

    planes = pl.pallas_call(
        planes_kernel,
        out_shape=pltpu.VMEM((taps * rows + rows // 2, width), history.dtype),
        in_specs=[ANY],
        out_specs=VMEM,
        scratch_shapes=[pltpu.SemaphoreType.DMA((taps + 1,))],
        compiler_params=SMALL,
        name="own_planes",
    )(far(history))
    *ends, tiles, meta = pl.pallas_call(
        functools.partial(table_kernel, slots, news, sites, groups),
        out_shape=[pltpu.VMEM((pairs // PIECES, rows, cols), tiles.dtype)] * PIECES
        + [pltpu.VMEM(tiles.shape, tiles.dtype), pltpu.SMEM((5, pairs), jnp.int32)],
        in_specs=[ANY] * 4,
        out_specs=[VMEM] * (PIECES + 1) + [SMEM],
        scratch_shapes=[
            pltpu.SMEM((1, pairs), jnp.int32),
            pltpu.SMEM((1, pairs), jnp.int32),
            pltpu.SemaphoreType.DMA((3 + pairs,)),
        ],
        compiler_params=SMALL,
        name="table",
    )(far(pair_src), far(pair_delay), far(tiles), planes)

    own = [planes] + [send(planes, *[("own", t)] * 2) for t in range(1, groups)]
    partners = [send(planes, *[(kind, 0) for kind in pair]) for pair in swaps[0]]
    tops = cut(partners, 0, HEAD)
    relayed = []
    for x in own[1:]:
        rest = cut([x], HEAD, x.shape[0] - HEAD)
        relayed.append(send(tops, *[("own", len(relayed) // 3 + 1)] * 2))
        relayed += [send(rest, *[(kind, 0) for kind in pair]) for pair in swaps[1]]
    pieces = [swap_cores(x) for x in ends]

    near = own + partners
    acc = near_part(meta, tiles, near)
    cross, halves, newest, acc = swapped_part(meta, tiles, acc, near, pieces)
    mine0, mine1 = relayed_part(
        meta, tiles, cross, halves, acc, relayed, groups + 2
    )

    strike, inverse, wave = held(strike_seg[None, :]), held(inverse), held(waveform)
    current0 = pl.pallas_call(
        first_kernel,
        out_shape=pltpu.VMEM((rows, width), jnp.bfloat16),
        in_specs=[SMEM] + [VMEM] * 5,
        out_specs=VMEM,
        compiler_params=SMALL,
        name="first_currents",
    )(table(meta), held(mine0), held(swap_cores(mine0)), inverse, strike, wave)

    fresh = [send(current0, *messages) for messages in rounds]
    for number, block in enumerate([current0] + fresh):
        mine1 = fresh_part(meta, newest, block, number, mine1)

    currents = pl.pallas_call(
        second_kernel,
        out_shape=jax.ShapeDtypeStruct((2, rows, width), jnp.bfloat16),
        in_specs=[SMEM] + [VMEM] * 6,
        out_specs=VMEM,
        compiler_params=SMALL,
        name="second_currents",
    )(
        table(meta),
        held(current0),
        held(mine1),
        held(swap_cores(mine1)),
        inverse,
        strike,
        wave,
    )
    return currents[None]


def solution(mesh):
    in_specs = (
        P(("site", "structur"), None, "sub", None, None),
        P(("scenario", "site", "structur"), None, None, None),
        P(("site", "structur"), None, None),
        P(("site", "structur"), None),
        P(("site", "structur"), None),
        P("scenario"),
        P("scenario", None),
    )
    out_specs = P(("scenario", "site", "structur"), None, None, None)
    return jax.shard_map(
        per_device, mesh=mesh, in_specs=in_specs, out_specs=out_specs, check_vma=False
    )
```

```python
import functools
import itertools

import jax
import jax.numpy as jnp
from jax import lax
from jax.experimental import pallas as pl
from jax.experimental.pallas import tpu as pltpu
from jax.sharding import PartitionSpec as P

GRID_AXES = ("site", "structur", "sub")
ALL_AXES = ("scenario",) + GRID_AXES
SMEM = pl.BlockSpec(memory_space=pltpu.SMEM)
VMEM = pl.BlockSpec(memory_space=pltpu.VMEM)
ANY = pl.BlockSpec(memory_space=pl.ANY)
SMALL = pltpu.CompilerParams(vmem_limit_bytes=4 << 20)

SLOT, LATE, NEWS, ORDER, PLACE = range(5)
CHUNK = 2
PIECES = 4
HEAD = 96


def held(x):
    return pltpu.with_memory_space_constraint(x, pltpu.VMEM)


def far(x):
    return pltpu.with_memory_space_constraint(x, pltpu.HBM)


def table(x):
    return pltpu.with_memory_space_constraint(x, pltpu.SMEM)


def partner_site(site, kind, sites):
    other = site ^ 1 if kind == "even" else (site + 1 if site % 2 else site - 1)
    return other if 0 <= other < sites else None


def link_pairs(kind, turn, sites, groups):
    pairs = []
    for site in range(sites):
        to_site = site if kind == "own" else partner_site(site, kind, sites)
        if to_site is None:
            continue
        for member in range(groups):
            pairs.append(
                (site * groups + member, to_site * groups + (member - turn) % groups)
            )
    return pairs


def swap_cores(x):
    return lax.ppermute(x, "sub", [(0, 1), (1, 0)])


def planes_kernel(history, planes, sem):
    core = lax.axis_index("sub")
    count, rows, _ = history.shape
    taps, half = count // 2, rows // 2
    copies = [
        pltpu.make_async_copy(
            history.at[core * taps + n], planes.at[pl.ds(n * rows, rows)], sem.at[n]
        )
        for n in range(taps)
    ]
    copies.append(
        pltpu.make_async_copy(
            history.at[count - 1, pl.ds(core * half, half)],
            planes.at[pl.ds(taps * rows, half)],
            sem.at[taps],
        )
    )
    for copy in copies:
        copy.start()
    for copy in copies:
        copy.wait()


def table_kernel(slots, news, sites, groups, *refs):
    src, delay, tiles, after = refs[:4]
    *ends, whole, meta, src_buf, delay_buf, sem = refs[4:]
    part = ends[0].shape[0]
    site, member, core = (lax.axis_index(a) for a in GRID_AXES)
    rows = tiles.shape[2]
    copies = [
        pltpu.make_async_copy(src, src_buf, sem.at[0]),
        pltpu.make_async_copy(delay, delay_buf, sem.at[1]),
        pltpu.make_async_copy(tiles, whole, sem.at[2]),
    ]
    for copy in copies:
        copy.start()
    copies[0].wait()
    copies[1].wait()
    last = tiles.shape[1] - 1
    for p in range(src.shape[1]):
        copies.append(
            pltpu.make_async_copy(
                tiles.at[p, jnp.where(delay_buf[0, p] == 1, 0, last)],
                ends[p // part].at[p % part],
                sem.at[3 + p],
            )
        )
        copies[-1].start()
    even_step = jnp.where(site % 2 == 0, 1, -1)
    ahead = jnp.int32(0)
    behind = jnp.int32(src.shape[1])
    for p in range(src.shape[1]):
        value, wait = src_buf[0, p], delay_buf[0, p]
        turn = (value % groups - member + groups) % groups
        dist = value // groups - site
        kind = jnp.where(dist == 0, 2, jnp.where(dist == even_step, 1, 0))
        key = kind * groups + turn
        slot, fresh = jnp.int32(-1), jnp.int32(-1)
        for n in range(3 * groups):
            mine = [jnp.where(core == 0, t[0][n], t[1][n]) for t in (slots, news)]
            slot = jnp.where(key == n, mine[0], slot)
            fresh = jnp.where(key == n, mine[1], fresh)
        meta[SLOT, p] = slot
        meta[LATE, p] = wait - 1
        meta[NEWS, p] = jnp.where(wait == 1, fresh, -1)
        relayed = slot >= groups + 2
        behind = behind - jnp.where(relayed, 0, 1)
        meta[ORDER, jnp.where(relayed, ahead, behind)] = p
        ahead = ahead + jnp.where(relayed, 1, 0)
        meta[PLACE, p] = core
    meta[PLACE, 0] = (site * groups + member) * rows
    meta[PLACE, 2] = ahead
    for copy in copies[2:]:
        copy.wait()


def swapped_kernel(count, meta, tiles, acc, *refs):
    sources, pieces = refs[:count], refs[count:-2]
    extra, total = refs[-2:]
    part = pieces[0].shape[0]
    taps, rows = tiles.shape[1:3]
    half, width = rows // 2, sources[0].shape[1]
    core = meta[PLACE, 1]
    total[...] = acc[...]
    for n, piece in enumerate(pieces):
        extra[n * part : (n + 1) * part] = piece[...]

    def add(step, left, right):
        total[:, step * width : (step + 1) * width] += jnp.dot(
            left, right, preferred_element_type=jnp.float32
        )

    def one(p, source):
        late = meta[LATE, p]

        @pl.when((late == 0) & (core == 0))
        def _():
            add(1, extra[p], source[(taps - 1) * rows : taps * rows])

        @pl.when((late == 1) & (core == 0))
        def _():
            add(0, extra[p, :, :half], source[taps * rows :])

        @pl.when((late == 1) & (core == 1))
        def _():
            add(0, extra[p], source[:rows])
            add(0, tiles[p, taps - 1, :, half:], source[taps * rows :])

    @pl.loop(0, tiles.shape[0])
    def _(p):
        @pl.when((meta[LATE, p] == 1) | (core == 0))
        def _():
            for slot, source in enumerate(sources):
                pl.when(meta[SLOT, p] == slot)(functools.partial(one, p, source))


def swapped_part(meta, tiles, acc, sources, pieces):
    pairs, _, rows, cols = tiles.shape
    return pl.pallas_call(
        functools.partial(swapped_kernel, len(sources)),
        out_shape=[
            pltpu.VMEM((pairs, rows, cols), tiles.dtype),
            pltpu.VMEM(acc.shape, acc.dtype),
        ],
        in_specs=[SMEM] + [VMEM] * (2 + len(sources) + len(pieces)),
        out_specs=[VMEM] * 2,
        compiler_params=SMALL,
        name="swapped_part",
    )(table(meta), held(tiles), held(acc), *[held(x) for x in sources + pieces])


def cut_kernel(start, count, *refs):
    sources, out = refs[:-1], refs[-1]
    for n, source in enumerate(sources):
        out[n * count : (n + 1) * count] = source[start : start + count]


def cut(sources, start, count):
    width = sources[0].shape[1]
    return pl.pallas_call(
        functools.partial(cut_kernel, start, count),
        out_shape=pltpu.VMEM((len(sources) * count, width), sources[0].dtype),
        in_specs=[VMEM] * len(sources),
        out_specs=VMEM,
        compiler_params=SMALL,
        name="cut",
    )(*[held(x) for x in sources])


def near_kernel(count, meta, tiles, *refs):
    sources, (total,) = refs[:count], refs[count:]
    taps, rows = tiles.shape[1:3]
    total[...] = jnp.zeros_like(total)

    def one(p, source):
        late = meta[LATE, p]
        planes = [source[k * rows : (k + 1) * rows] for k in range(taps)]
        empty = jnp.zeros_like(planes[0])
        planes = [empty] + planes + [empty]
        both = [
            jnp.concatenate(
                [
                    jnp.where(late == 1, planes[k + 2], planes[k + 1]),
                    jnp.where(late == 1, planes[k + 1], planes[k]),
                ],
                axis=1,
            )
            for k in range(taps)
        ]
        total[...] += jnp.dot(
            jnp.concatenate([tiles[p, k] for k in range(taps)], axis=1),
            jnp.concatenate(both, axis=0),
            preferred_element_type=jnp.float32,
        )

    @pl.loop(0, tiles.shape[0])
    def _(p):
        for slot, source in enumerate(sources):
            pl.when(meta[SLOT, p] == slot)(functools.partial(one, p, source))


def near_part(meta, tiles, sources):
    rows, width = tiles.shape[2], sources[0].shape[1]
    return pl.pallas_call(
        functools.partial(near_kernel, len(sources)),
        out_shape=pltpu.VMEM((rows, 2 * width), jnp.float32),
        in_specs=[SMEM] + [VMEM] * (1 + len(sources)),
        out_specs=VMEM,
        compiler_params=SMALL,
        name="near_part",
    )(table(meta), held(tiles), *[held(x) for x in sources])


def relayed_kernel(first, turns, meta, tiles, extra, acc, *refs):
    sources, (out0, out1, total, store) = refs[: 3 * turns], refs[3 * turns :]
    pairs, taps, rows = tiles.shape[:3]
    half, width = rows // 2, acc.shape[1] // 2
    held_rows = taps * rows
    block = held_rows + 3 * half
    none = 2 * turns * block
    core = meta[PLACE, 1]
    empty = jnp.zeros((half, width), store.dtype)
    for turn in range(turns):
        tops, *rests = sources[3 * turn : 3 * turn + 3]
        for n, rest in enumerate(rests):
            base = (2 * turn + n) * block
            store[base : base + HEAD] = tops[n * HEAD : (n + 1) * HEAD]
            store[base + HEAD : base + held_rows] = rest[: held_rows - HEAD]
            store[base + held_rows : base + held_rows + half] = empty
            store[base + held_rows + half : base + block - half] = rest[held_rows - HEAD :]
            store[base + block - half : base + block] = empty
    store[none:] = jnp.zeros((rows, width), store.dtype)
    total[...] = acc[...]

    def pair(a, b):
        return jnp.concatenate(
            [store[pl.ds(pl.multiple_of(at, half), rows)] for at in (a, b)], axis=1
        )

    def chunk(start):
        lefts, rights = [], []
        for i in range(start, start + CHUNK):
            p = meta[ORDER, i]
            used = i < meta[PLACE, 2]
            late = meta[LATE, p]
            base = (meta[SLOT, p] - first) * block
            early = jnp.logical_and(used, late == 0)
            after = jnp.logical_and(used, late == 1)
            ats = [jnp.where(used, base + k * rows, none) for k in range(taps)]
            last = jnp.where(jnp.logical_and(after, core == 1), base + held_rows, none)
            before = [none] + ats + [last]
            for k in range(taps):
                lefts.append(tiles[p, k])
                a = jnp.where(late == 1, before[k + 2], before[k + 1])
                b = jnp.where(late == 1, before[k + 1], before[k])
                rights.append(pair(a, b))
            lefts.append(extra[p])
            a = jnp.where(core == 0, base + held_rows + half, base)
            b = jnp.where(jnp.logical_and(early, core == 0), ats[taps - 1], none)
            rights.append(pair(jnp.where(after, a, none), b))
        total[...] += jnp.dot(
            jnp.concatenate(lefts, axis=1),
            jnp.concatenate(rights, axis=0),
            preferred_element_type=jnp.float32,
        )

    for start in range(0, pairs, CHUNK):
        pl.when(meta[PLACE, 2] > start)(functools.partial(chunk, start))
    out0[...] = total[:, :width]
    out1[...] = total[:, width:]


def relayed_part(meta, tiles, extra, acc, sources, first):
    taps, rows = tiles.shape[1:3]
    width, turns = acc.shape[1] // 2, len(sources) // 3
    store = (2 * turns * (taps * rows + 3 * rows // 2) + rows, width)
    half = pltpu.VMEM((rows, width), jnp.float32)
    room = 2 * store[0] * width + 4 * acc.size
    return pl.pallas_call(
        functools.partial(relayed_kernel, first, turns),
        out_shape=[half, half],
        in_specs=[SMEM] + [VMEM] * (3 + len(sources)),
        out_specs=[VMEM, VMEM],
        scratch_shapes=[
            pltpu.VMEM(acc.shape, acc.dtype),
            pltpu.VMEM(store, sources[0].dtype),
        ],
        compiler_params=pltpu.CompilerParams(vmem_limit_bytes=room + (4 << 20)),
        name="relayed_part",
    )(
        table(meta),
        held(tiles),
        held(extra),
        held(acc),
        *[held(x) for x in sources],
    )


def solve_rows(base, mine, other, inverse, strike, wave):
    rows, width = mine.shape
    segments = base + lax.broadcasted_iota(jnp.int32, (rows, width), 0)
    incident = jnp.where(segments == strike, wave, jnp.float32(0.0))
    rhs = (incident - (mine + other)).astype(jnp.bfloat16)
    return jnp.dot(inverse, rhs, preferred_element_type=jnp.float32).astype(
        jnp.bfloat16
    )


def first_kernel(meta, mine, other, inverse, strike, wave, out):
    out[...] = solve_rows(
        meta[PLACE, 0], mine[...], other[...], inverse[...], strike[...], wave[0:1, :]
    )


def second_kernel(meta, first, mine, other, inverse, strike, wave, out):
    out[0] = first[...]
    out[1] = solve_rows(
        meta[PLACE, 0], mine[...], other[...], inverse[...], strike[...], wave[1:2, :]
    )


def fresh_kernel(number, meta, tiles, extra, source, acc, out):
    out[...] = acc[...]

    def add(tile):
        out[...] += jnp.dot(tile, source[...], preferred_element_type=jnp.float32)

    @pl.loop(0, tiles.shape[0])
    def _(p):
        @pl.when(meta[NEWS, p] == number)
        def _():
            pl.when(meta[PLACE, 1] == 0)(lambda: add(tiles[p, 0]))
            pl.when(meta[PLACE, 1] == 1)(lambda: add(extra[p]))


def fresh_part(meta, tiles, extra, source, number, acc):
    return pl.pallas_call(
        functools.partial(fresh_kernel, number),
        out_shape=pltpu.VMEM(acc.shape, acc.dtype),
        in_specs=[SMEM] + [VMEM] * 4,
        out_specs=VMEM,
        compiler_params=SMALL,
        name="fresh_part",
    )(table(meta), held(tiles), held(extra), held(source), held(acc))


def per_device(tiles, history, self_inverse, pair_src, pair_delay, strike_seg, waveform):
    sites, groups = lax.axis_size("site"), lax.axis_size("structur")
    tiles, history, inverse = tiles[0], history[0], self_inverse[0]
    pairs, taps, rows, cols = tiles.shape
    width = history.shape[2]

    kinds = ("odd", "even", "own")
    key = {(k, t): n * groups + t for n, k in enumerate(kinds) for t in range(groups)}

    def send(x, *messages):
        scenarios, grid = lax.axis_size("scenario"), sites * groups * 2
        pairs = []
        for scenario in range(scenarios):
            twin = scenario ^ 1
            for c, m in enumerate(messages):
                moves = dict(link_pairs(*m, sites, groups)) if m else {}
                for a in range(sites * groups):
                    source = scenario * grid + 2 * a + c
                    if a in moves:
                        pairs.append((source, scenario * grid + 2 * moves[a] + c))
                    elif twin < scenarios:
                        pairs.append((source, twin * grid + 2 * a + c))
        return lax.ppermute(x, ALL_AXES, pairs)

    swaps = ((("even", "odd"), ("odd", "even")), (("even", "odd"), ("odd", "even")))
    slots = [[-1] * (3 * groups) for _ in range(2)]
    for c in range(2):
        for t in range(groups):
            slots[c][key["own", t]] = t
            for n, pair in enumerate(swaps[min(t, 1)]):
                slots[c][key[pair[c], t]] = groups + 2 * t + n

    straight = [("odd", 0)]+[("own", t) for t in range(1, groups)]+[("even", 0)]
    diagonal = [(kind, t) for t in range(1, groups) for kind in ("even", "odd")]
    while len(diagonal) > len(straight):
        straight.append(diagonal.pop())
    rounds = list(itertools.zip_longest(straight, diagonal))
    news = [[-1] * (3 * groups) for _ in range(2)]
    news[1][key["own", 0]] = 0
    for n, messages in enumerate(rounds):
        for c, m in enumerate(messages):
            if m is not None:
                news[c][key[m]] = 1 + n

    planes = pl.pallas_call(
        planes_kernel,
        out_shape=pltpu.VMEM((taps * rows + rows // 2, width), history.dtype),
        in_specs=[ANY],
        out_specs=VMEM,
        scratch_shapes=[pltpu.SemaphoreType.DMA((taps + 1,))],
        compiler_params=SMALL,
        name="own_planes",
    )(far(history))
    *ends, tiles, meta = pl.pallas_call(
        functools.partial(table_kernel, slots, news, sites, groups),
        out_shape=[pltpu.VMEM((pairs // PIECES, rows, cols), tiles.dtype)] * PIECES
        + [pltpu.VMEM(tiles.shape, tiles.dtype), pltpu.SMEM((5, pairs), jnp.int32)],
        in_specs=[ANY] * 4,
        out_specs=[VMEM] * (PIECES + 1) + [SMEM],
        scratch_shapes=[
            pltpu.SMEM((1, pairs), jnp.int32),
            pltpu.SMEM((1, pairs), jnp.int32),
            pltpu.SemaphoreType.DMA((3 + pairs,)),
        ],
        compiler_params=SMALL,
        name="table",
    )(far(pair_src), far(pair_delay), far(tiles), planes)

    own = [planes] + [send(planes, *[("own", t)] * 2) for t in range(1, groups)]
    partners = [send(planes, *[(kind, 0) for kind in pair]) for pair in swaps[0]]
    tops = cut(partners, 0, HEAD)
    relayed = []
    for x in own[1:]:
        rest = cut([x], HEAD, x.shape[0] - HEAD)
        relayed.append(send(tops, *[("own", len(relayed) // 3 + 1)] * 2))
        relayed += [send(rest, *[(kind, 0) for kind in pair]) for pair in swaps[1]]
    pieces = [swap_cores(x) for x in ends]

    near = own + partners
    acc = near_part(meta, tiles, near)
    extra, acc = swapped_part(meta, tiles, acc, near, pieces)
    mine0, mine1 = relayed_part(meta, tiles, extra, acc, relayed, groups + 2)

    strike, inverse, wave = held(strike_seg[None, :]), held(inverse), held(waveform)
    current0 = pl.pallas_call(
        first_kernel,
        out_shape=pltpu.VMEM((rows, width), jnp.bfloat16),
        in_specs=[SMEM] + [VMEM] * 5,
        out_specs=VMEM,
        compiler_params=SMALL,
        name="first_currents",
    )(table(meta), held(mine0), held(swap_cores(mine0)), inverse, strike, wave)

    fresh = [send(current0, *messages) for messages in rounds]
    for number, block in enumerate([current0] + fresh):
        mine1 = fresh_part(meta, tiles, extra, block, number, mine1)

    currents = pl.pallas_call(
        second_kernel,
        out_shape=jax.ShapeDtypeStruct((2, rows, width), jnp.bfloat16),
        in_specs=[SMEM] + [VMEM] * 6,
        out_specs=VMEM,
        compiler_params=SMALL,
        name="second_currents",
    )(
        table(meta),
        held(current0),
        held(mine1),
        held(swap_cores(mine1)),
        inverse,
        strike,
        wave,
    )
    return currents[None]


def solution(mesh):
    in_specs = (
        P(("site", "structur"), None, "sub", None, None),
        P(("scenario", "site", "structur"), None, None, None),
        P(("site", "structur"), None, None),
        P(("site", "structur"), None),
        P(("site", "structur"), None),
        P("scenario"),
        P("scenario", None),
    )
    out_specs = P(("scenario", "site", "structur"), None, None, None)
    return jax.shard_map(
        per_device, mesh=mesh, in_specs=in_specs, out_specs=out_specs, check_vma=False
    )
```

```python
import functools
import itertools

import jax
import jax.numpy as jnp
from jax import lax
from jax.experimental import pallas as pl
from jax.experimental.pallas import tpu as pltpu
from jax.sharding import PartitionSpec as P

GRID_AXES = ("site", "structur", "sub")
ALL_AXES = ("scenario",) + GRID_AXES
SMEM = pl.BlockSpec(memory_space=pltpu.SMEM)
VMEM = pl.BlockSpec(memory_space=pltpu.VMEM)
ANY = pl.BlockSpec(memory_space=pl.ANY)
SMALL = pltpu.CompilerParams(vmem_limit_bytes=4 << 20)

SLOT, LATE, NEWS, ORDER, PLACE = range(5)
CHUNK = 2
PIECES = 4
HEAD = 112


def held(x):
    return pltpu.with_memory_space_constraint(x, pltpu.VMEM)


def far(x):
    return pltpu.with_memory_space_constraint(x, pltpu.HBM)


def table(x):
    return pltpu.with_memory_space_constraint(x, pltpu.SMEM)


def partner_site(site, kind, sites):
    other = site ^ 1 if kind == "even" else (site + 1 if site % 2 else site - 1)
    return other if 0 <= other < sites else None


def link_pairs(kind, turn, sites, groups):
    pairs = []
    for site in range(sites):
        to_site = site if kind == "own" else partner_site(site, kind, sites)
        if to_site is None:
            continue
        for member in range(groups):
            pairs.append(
                (site * groups + member, to_site * groups + (member - turn) % groups)
            )
    return pairs


def swap_cores(x):
    return lax.ppermute(x, "sub", [(0, 1), (1, 0)])


def planes_kernel(history, planes, sem):
    core = lax.axis_index("sub")
    count, rows, _ = history.shape
    taps, half = count // 2, rows // 2
    copies = [
        pltpu.make_async_copy(
            history.at[core * taps + n], planes.at[pl.ds(n * rows, rows)], sem.at[n]
        )
        for n in range(taps)
    ]
    copies.append(
        pltpu.make_async_copy(
            history.at[count - 1, pl.ds(core * half, half)],
            planes.at[pl.ds(taps * rows, half)],
            sem.at[taps],
        )
    )
    for copy in copies:
        copy.start()
    for copy in copies:
        copy.wait()


def table_kernel(slots, news, sites, groups, *refs):
    src, delay, tiles, after = refs[:4]
    *ends, whole, meta, src_buf, delay_buf, sem = refs[4:]
    part = ends[0].shape[0]
    site, member, core = (lax.axis_index(a) for a in GRID_AXES)
    rows = tiles.shape[2]
    copies = [
        pltpu.make_async_copy(src, src_buf, sem.at[0]),
        pltpu.make_async_copy(delay, delay_buf, sem.at[1]),
        pltpu.make_async_copy(tiles, whole, sem.at[2]),
    ]
    for copy in copies:
        copy.start()
    copies[0].wait()
    copies[1].wait()
    last = tiles.shape[1] - 1
    for p in range(src.shape[1]):
        copies.append(
            pltpu.make_async_copy(
                tiles.at[p, jnp.where(delay_buf[0, p] == 1, 0, last)],
                ends[p // part].at[p % part],
                sem.at[3 + p],
            )
        )
        copies[-1].start()
    even_step = jnp.where(site % 2 == 0, 1, -1)
    ahead = jnp.int32(0)
    behind = jnp.int32(src.shape[1])
    for p in range(src.shape[1]):
        value, wait = src_buf[0, p], delay_buf[0, p]
        turn = (value % groups - member + groups) % groups
        dist = value // groups - site
        kind = jnp.where(dist == 0, 2, jnp.where(dist == even_step, 1, 0))
        key = kind * groups + turn
        slot, fresh = jnp.int32(-1), jnp.int32(-1)
        for n in range(3 * groups):
            mine = [jnp.where(core == 0, t[0][n], t[1][n]) for t in (slots, news)]
            slot = jnp.where(key == n, mine[0], slot)
            fresh = jnp.where(key == n, mine[1], fresh)
        meta[SLOT, p] = slot
        meta[LATE, p] = wait - 1
        meta[NEWS, p] = jnp.where(wait == 1, fresh, -1)
        relayed = slot >= groups + 2
        behind = behind - jnp.where(relayed, 0, 1)
        meta[ORDER, jnp.where(relayed, ahead, behind)] = p
        ahead = ahead + jnp.where(relayed, 1, 0)
        meta[PLACE, p] = core
    meta[PLACE, 0] = (site * groups + member) * rows
    meta[PLACE, 2] = ahead
    for copy in copies[2:]:
        copy.wait()


def swapped_kernel(count, meta, tiles, acc, *refs):
    sources, pieces = refs[:count], refs[count:-2]
    extra, total = refs[-2:]
    part = pieces[0].shape[0]
    taps, rows = tiles.shape[1:3]
    half, width = rows // 2, sources[0].shape[1]
    core = meta[PLACE, 1]
    total[...] = acc[...]
    for n, piece in enumerate(pieces):
        extra[n * part : (n + 1) * part] = piece[...]

    def add(step, left, right):
        total[:, step * width : (step + 1) * width] += jnp.dot(
            left, right, preferred_element_type=jnp.float32
        )

    def one(p, source):
        late = meta[LATE, p]

        @pl.when((late == 0) & (core == 0))
        def _():
            add(1, extra[p], source[(taps - 1) * rows : taps * rows])

        @pl.when((late == 1) & (core == 0))
        def _():
            add(0, extra[p, :, :half], source[taps * rows :])

        @pl.when((late == 1) & (core == 1))
        def _():
            add(0, extra[p], source[:rows])
            add(0, tiles[p, taps - 1, :, half:], source[taps * rows :])

    @pl.loop(0, tiles.shape[0])
    def _(p):
        @pl.when((meta[LATE, p] == 1) | (core == 0))
        def _():
            for slot, source in enumerate(sources):
                pl.when(meta[SLOT, p] == slot)(functools.partial(one, p, source))


def swapped_part(meta, tiles, acc, sources, pieces):
    pairs, _, rows, cols = tiles.shape
    return pl.pallas_call(
        functools.partial(swapped_kernel, len(sources)),
        out_shape=[
            pltpu.VMEM((pairs, rows, cols), tiles.dtype),
            pltpu.VMEM(acc.shape, acc.dtype),
        ],
        in_specs=[SMEM] + [VMEM] * (2 + len(sources) + len(pieces)),
        out_specs=[VMEM] * 2,
        compiler_params=SMALL,
        name="swapped_part",
    )(table(meta), held(tiles), held(acc), *[held(x) for x in sources + pieces])


def cut_kernel(start, count, *refs):
    sources, out = refs[:-1], refs[-1]
    for n, source in enumerate(sources):
        out[n * count : (n + 1) * count] = source[start : start + count]


def cut(sources, start, count):
    width = sources[0].shape[1]
    return pl.pallas_call(
        functools.partial(cut_kernel, start, count),
        out_shape=pltpu.VMEM((len(sources) * count, width), sources[0].dtype),
        in_specs=[VMEM] * len(sources),
        out_specs=VMEM,
        compiler_params=SMALL,
        name="cut",
    )(*[held(x) for x in sources])


def near_kernel(count, meta, tiles, *refs):
    sources, (total,) = refs[:count], refs[count:]
    taps, rows = tiles.shape[1:3]
    total[...] = jnp.zeros_like(total)

    def one(p, source):
        late = meta[LATE, p]
        planes = [source[k * rows : (k + 1) * rows] for k in range(taps)]
        empty = jnp.zeros_like(planes[0])
        planes = [empty] + planes + [empty]
        both = [
            jnp.concatenate(
                [
                    jnp.where(late == 1, planes[k + 2], planes[k + 1]),
                    jnp.where(late == 1, planes[k + 1], planes[k]),
                ],
                axis=1,
            )
            for k in range(taps)
        ]
        total[...] += jnp.dot(
            jnp.concatenate([tiles[p, k] for k in range(taps)], axis=1),
            jnp.concatenate(both, axis=0),
            preferred_element_type=jnp.float32,
        )

    @pl.loop(0, tiles.shape[0])
    def _(p):
        for slot, source in enumerate(sources):
            pl.when(meta[SLOT, p] == slot)(functools.partial(one, p, source))


def near_part(meta, tiles, sources):
    rows, width = tiles.shape[2], sources[0].shape[1]
    return pl.pallas_call(
        functools.partial(near_kernel, len(sources)),
        out_shape=pltpu.VMEM((rows, 2 * width), jnp.float32),
        in_specs=[SMEM] + [VMEM] * (1 + len(sources)),
        out_specs=VMEM,
        compiler_params=SMALL,
        name="near_part",
    )(table(meta), held(tiles), *[held(x) for x in sources])


def relayed_kernel(first, turns, meta, tiles, extra, acc, *refs):
    sources, (out0, out1, total, store) = refs[: 3 * turns], refs[3 * turns :]
    pairs, taps, rows = tiles.shape[:3]
    half, width = rows // 2, acc.shape[1] // 2
    held_rows = taps * rows
    block = held_rows + 3 * half
    none = 2 * turns * block
    core = meta[PLACE, 1]
    empty = jnp.zeros((half, width), store.dtype)
    for turn in range(turns):
        tops, *rests = sources[3 * turn : 3 * turn + 3]
        for n, rest in enumerate(rests):
            base = (2 * turn + n) * block
            store[base : base + HEAD] = tops[n * HEAD : (n + 1) * HEAD]
            store[base + HEAD : base + held_rows] = rest[: held_rows - HEAD]
            store[base + held_rows : base + held_rows + half] = empty
            store[base + held_rows + half : base + block - half] = rest[held_rows - HEAD :]
            store[base + block - half : base + block] = empty
    store[none:] = jnp.zeros((rows, width), store.dtype)
    total[...] = acc[...]

    def pair(a, b):
        return jnp.concatenate(
            [store[pl.ds(pl.multiple_of(at, half), rows)] for at in (a, b)], axis=1
        )

    def chunk(start):
        lefts, rights = [], []
        for i in range(start, start + CHUNK):
            p = meta[ORDER, i]
            used = i < meta[PLACE, 2]
            late = meta[LATE, p]
            base = (meta[SLOT, p] - first) * block
            early = jnp.logical_and(used, late == 0)
            after = jnp.logical_and(used, late == 1)
            ats = [jnp.where(used, base + k * rows, none) for k in range(taps)]
            last = jnp.where(jnp.logical_and(after, core == 1), base + held_rows, none)
            before = [none] + ats + [last]
            for k in range(taps):
                lefts.append(tiles[p, k])
                a = jnp.where(late == 1, before[k + 2], before[k + 1])
                b = jnp.where(late == 1, before[k + 1], before[k])
                rights.append(pair(a, b))
            lefts.append(extra[p])
            a = jnp.where(core == 0, base + held_rows + half, base)
            b = jnp.where(jnp.logical_and(early, core == 0), ats[taps - 1], none)
            rights.append(pair(jnp.where(after, a, none), b))
        total[...] += jnp.dot(
            jnp.concatenate(lefts, axis=1),
            jnp.concatenate(rights, axis=0),
            preferred_element_type=jnp.float32,
        )

    for start in range(0, pairs, CHUNK):
        pl.when(meta[PLACE, 2] > start)(functools.partial(chunk, start))
    out0[...] = total[:, :width]
    out1[...] = total[:, width:]


def relayed_part(meta, tiles, extra, acc, sources, first):
    taps, rows = tiles.shape[1:3]
    width, turns = acc.shape[1] // 2, len(sources) // 3
    store = (2 * turns * (taps * rows + 3 * rows // 2) + rows, width)
    half = pltpu.VMEM((rows, width), jnp.float32)
    room = 2 * store[0] * width + 4 * acc.size
    return pl.pallas_call(
        functools.partial(relayed_kernel, first, turns),
        out_shape=[half, half],
        in_specs=[SMEM] + [VMEM] * (3 + len(sources)),
        out_specs=[VMEM, VMEM],
        scratch_shapes=[
            pltpu.VMEM(acc.shape, acc.dtype),
            pltpu.VMEM(store, sources[0].dtype),
        ],
        compiler_params=pltpu.CompilerParams(vmem_limit_bytes=room + (4 << 20)),
        name="relayed_part",
    )(
        table(meta),
        held(tiles),
        held(extra),
        held(acc),
        *[held(x) for x in sources],
    )


def solve_rows(base, mine, other, inverse, strike, wave):
    rows, width = mine.shape
    segments = base + lax.broadcasted_iota(jnp.int32, (rows, width), 0)
    incident = jnp.where(segments == strike, wave, jnp.float32(0.0))
    rhs = (incident - (mine + other)).astype(jnp.bfloat16)
    return jnp.dot(inverse, rhs, preferred_element_type=jnp.float32).astype(
        jnp.bfloat16
    )


def first_kernel(meta, mine, other, inverse, strike, wave, out):
    out[...] = solve_rows(
        meta[PLACE, 0], mine[...], other[...], inverse[...], strike[...], wave[0:1, :]
    )


def second_kernel(meta, first, mine, other, inverse, strike, wave, out):
    out[0] = first[...]
    out[1] = solve_rows(
        meta[PLACE, 0], mine[...], other[...], inverse[...], strike[...], wave[1:2, :]
    )


def fresh_kernel(number, meta, tiles, extra, source, acc, out):
    def add(tile):
        out[...] += jnp.dot(tile, source[...], preferred_element_type=jnp.float32)

    @pl.loop(0, tiles.shape[0])
    def _(p):
        @pl.when(meta[NEWS, p] == number)
        def _():
            pl.when(meta[PLACE, 1] == 0)(lambda: add(tiles[p, 0]))
            pl.when(meta[PLACE, 1] == 1)(lambda: add(extra[p]))


def fresh_part(meta, tiles, extra, source, number, acc):
    return pl.pallas_call(
        functools.partial(fresh_kernel, number),
        out_shape=pltpu.VMEM(acc.shape, acc.dtype),
        in_specs=[SMEM] + [VMEM] * 4,
        out_specs=VMEM,
        input_output_aliases={4: 0},
        compiler_params=SMALL,
        name="fresh_part",
    )(table(meta), held(tiles), held(extra), held(source), held(acc))


def per_device(tiles, history, self_inverse, pair_src, pair_delay, strike_seg, waveform):
    sites, groups = lax.axis_size("site"), lax.axis_size("structur")
    tiles, history, inverse = tiles[0], history[0], self_inverse[0]
    pairs, taps, rows, cols = tiles.shape
    width = history.shape[2]

    kinds = ("odd", "even", "own")
    key = {(k, t): n * groups + t for n, k in enumerate(kinds) for t in range(groups)}

    def send(x, *messages):
        scenarios, grid = lax.axis_size("scenario"), sites * groups * 2
        pairs = []
        for scenario in range(scenarios):
            twin = scenario ^ 1
            for c, m in enumerate(messages):
                moves = dict(link_pairs(*m, sites, groups)) if m else {}
                for a in range(sites * groups):
                    source = scenario * grid + 2 * a + c
                    if a in moves:
                        pairs.append((source, scenario * grid + 2 * moves[a] + c))
                    elif twin < scenarios:
                        pairs.append((source, twin * grid + 2 * a + c))
        return lax.ppermute(x, ALL_AXES, pairs)

    swaps = ((("even", "odd"), ("odd", "even")), (("even", "odd"), ("odd", "even")))
    slots = [[-1] * (3 * groups) for _ in range(2)]
    for c in range(2):
        for t in range(groups):
            slots[c][key["own", t]] = t
            for n, pair in enumerate(swaps[min(t, 1)]):
                slots[c][key[pair[c], t]] = groups + 2 * t + n

    straight = [("odd", 0)]+[("own", t) for t in range(1, groups)]+[("even", 0)]
    diagonal = [(kind, t) for t in range(1, groups) for kind in ("even", "odd")]
    while len(diagonal) > len(straight):
        straight.append(diagonal.pop())
    rounds = list(itertools.zip_longest(straight, diagonal))
    news = [[-1] * (3 * groups) for _ in range(2)]
    news[1][key["own", 0]] = 0
    for n, messages in enumerate(rounds):
        for c, m in enumerate(messages):
            if m is not None:
                news[c][key[m]] = 1 + n

    planes = pl.pallas_call(
        planes_kernel,
        out_shape=pltpu.VMEM((taps * rows + rows // 2, width), history.dtype),
        in_specs=[ANY],
        out_specs=VMEM,
        scratch_shapes=[pltpu.SemaphoreType.DMA((taps + 1,))],
        compiler_params=SMALL,
        name="own_planes",
    )(far(history))
    *ends, tiles, meta = pl.pallas_call(
        functools.partial(table_kernel, slots, news, sites, groups),
        out_shape=[pltpu.VMEM((pairs // PIECES, rows, cols), tiles.dtype)] * PIECES
        + [pltpu.VMEM(tiles.shape, tiles.dtype), pltpu.SMEM((5, pairs), jnp.int32)],
        in_specs=[ANY] * 4,
        out_specs=[VMEM] * (PIECES + 1) + [SMEM],
        scratch_shapes=[
            pltpu.SMEM((1, pairs), jnp.int32),
            pltpu.SMEM((1, pairs), jnp.int32),
            pltpu.SemaphoreType.DMA((3 + pairs,)),
        ],
        compiler_params=SMALL,
        name="table",
    )(far(pair_src), far(pair_delay), far(tiles), planes)

    own = [planes] + [send(planes, *[("own", t)] * 2) for t in range(1, groups)]
    partners = [send(planes, *[(kind, 0) for kind in pair]) for pair in swaps[0]]
    tops = cut(partners, 0, HEAD)
    relayed = []
    for x in own[1:]:
        rest = cut([x], HEAD, x.shape[0] - HEAD)
        relayed.append(send(tops, *[("own", len(relayed) // 3 + 1)] * 2))
        relayed += [send(rest, *[(kind, 0) for kind in pair]) for pair in swaps[1]]
    pieces = [swap_cores(x) for x in ends]

    near = own + partners
    acc = near_part(meta, tiles, near)
    extra, acc = swapped_part(meta, tiles, acc, near, pieces)
    mine0, mine1 = relayed_part(meta, tiles, extra, acc, relayed, groups + 2)

    strike, inverse, wave = held(strike_seg[None, :]), held(inverse), held(waveform)
    current0 = pl.pallas_call(
        first_kernel,
        out_shape=pltpu.VMEM((rows, width), jnp.bfloat16),
        in_specs=[SMEM] + [VMEM] * 5,
        out_specs=VMEM,
        compiler_params=SMALL,
        name="first_currents",
    )(table(meta), held(mine0), held(swap_cores(mine0)), inverse, strike, wave)

    fresh = [send(current0, *messages) for messages in rounds]
    for number, block in enumerate([current0] + fresh):
        mine1 = fresh_part(meta, tiles, extra, block, number, mine1)

    currents = pl.pallas_call(
        second_kernel,
        out_shape=jax.ShapeDtypeStruct((2, rows, width), jnp.bfloat16),
        in_specs=[SMEM] + [VMEM] * 6,
        out_specs=VMEM,
        compiler_params=SMALL,
        name="second_currents",
    )(
        table(meta),
        held(current0),
        held(mine1),
        held(swap_cores(mine1)),
        inverse,
        strike,
        wave,
    )
    return currents[None]


def solution(mesh):
    in_specs = (
        P(("site", "structur"), None, "sub", None, None),
        P(("scenario", "site", "structur"), None, None, None),
        P(("site", "structur"), None, None),
        P(("site", "structur"), None),
        P(("site", "structur"), None),
        P("scenario"),
        P("scenario", None),
    )
    out_specs = P(("scenario", "site", "structur"), None, None, None)
    return jax.shard_map(
        per_device, mesh=mesh, in_specs=in_specs, out_specs=out_specs, check_vma=False
    )
```

```python
import functools
import itertools

import jax
import jax.numpy as jnp
from jax import lax
from jax.experimental import pallas as pl
from jax.experimental.pallas import tpu as pltpu
from jax.sharding import PartitionSpec as P

GRID_AXES = ("site", "structur", "sub")
ALL_AXES = ("scenario",) + GRID_AXES
SMEM = pl.BlockSpec(memory_space=pltpu.SMEM)
VMEM = pl.BlockSpec(memory_space=pltpu.VMEM)
ANY = pl.BlockSpec(memory_space=pl.ANY)
SMALL = pltpu.CompilerParams(vmem_limit_bytes=4 << 20)

SLOT, LATE, NEWS, ORDER, PLACE = range(5)
CHUNK = 2
PIECES = 4
HEAD = 96


def held(x):
    return pltpu.with_memory_space_constraint(x, pltpu.VMEM)


def far(x):
    return pltpu.with_memory_space_constraint(x, pltpu.HBM)


def table(x):
    return pltpu.with_memory_space_constraint(x, pltpu.SMEM)


def partner_site(site, kind, sites):
    other = site ^ 1 if kind == "even" else (site + 1 if site % 2 else site - 1)
    return other if 0 <= other < sites else None


def link_pairs(kind, turn, sites, groups):
    pairs = []
    for site in range(sites):
        to_site = site if kind == "own" else partner_site(site, kind, sites)
        if to_site is None:
            continue
        for member in range(groups):
            pairs.append(
                (site * groups + member, to_site * groups + (member - turn) % groups)
            )
    return pairs


def swap_cores(x):
    return lax.ppermute(x, "sub", [(0, 1), (1, 0)])


def planes_kernel(history, planes, sem):
    core = lax.axis_index("sub")
    count, rows, _ = history.shape
    taps, half = count // 2, rows // 2
    copies = [
        pltpu.make_async_copy(
            history.at[core * taps + n], planes.at[pl.ds(n * rows, rows)], sem.at[n]
        )
        for n in range(taps)
    ]
    copies.append(
        pltpu.make_async_copy(
            history.at[count - 1, pl.ds(core * half, half)],
            planes.at[pl.ds(taps * rows, half)],
            sem.at[taps],
        )
    )
    for copy in copies:
        copy.start()
    for copy in copies:
        copy.wait()


def table_kernel(slots, news, sites, groups, *refs):
    src, delay, tiles, after = refs[:4]
    *ends, whole, meta, src_buf, delay_buf, sem = refs[4:]
    part = ends[0].shape[0]
    site, member, core = (lax.axis_index(a) for a in GRID_AXES)
    rows = tiles.shape[2]
    copies = [
        pltpu.make_async_copy(src, src_buf, sem.at[0]),
        pltpu.make_async_copy(delay, delay_buf, sem.at[1]),
        pltpu.make_async_copy(tiles, whole, sem.at[2]),
    ]
    for copy in copies:
        copy.start()
    copies[0].wait()
    copies[1].wait()
    last = tiles.shape[1] - 1
    for p in range(src.shape[1]):
        copies.append(
            pltpu.make_async_copy(
                tiles.at[p, jnp.where(delay_buf[0, p] == 1, 0, last)],
                ends[p // part].at[p % part],
                sem.at[3 + p],
            )
        )
        copies[-1].start()
    even_step = jnp.where(site % 2 == 0, 1, -1)
    ahead = jnp.int32(0)
    behind = jnp.int32(src.shape[1])
    for p in range(src.shape[1]):
        value, wait = src_buf[0, p], delay_buf[0, p]
        turn = (value % groups - member + groups) % groups
        dist = value // groups - site
        kind = jnp.where(dist == 0, 2, jnp.where(dist == even_step, 1, 0))
        key = kind * groups + turn
        slot, fresh = jnp.int32(-1), jnp.int32(-1)
        for n in range(3 * groups):
            mine = [jnp.where(core == 0, t[0][n], t[1][n]) for t in (slots, news)]
            slot = jnp.where(key == n, mine[0], slot)
            fresh = jnp.where(key == n, mine[1], fresh)
        meta[SLOT, p] = slot
        meta[LATE, p] = wait - 1
        meta[NEWS, p] = jnp.where(wait == 1, fresh, -1)
        relayed = slot >= groups + 2
        behind = behind - jnp.where(relayed, 0, 1)
        meta[ORDER, jnp.where(relayed, ahead, behind)] = p
        ahead = ahead + jnp.where(relayed, 1, 0)
        meta[PLACE, p] = core
    meta[PLACE, 0] = (site * groups + member) * rows
    meta[PLACE, 2] = ahead
    for copy in copies[2:]:
        copy.wait()


def swapped_kernel(count, meta, tiles, acc, *refs):
    sources, pieces = refs[:count], refs[count:-2]
    extra, total = refs[-2:]
    part = pieces[0].shape[0]
    taps, rows = tiles.shape[1:3]
    half, width = rows // 2, sources[0].shape[1]
    core = meta[PLACE, 1]
    total[...] = acc[...]
    for n, piece in enumerate(pieces):
        extra[n * part : (n + 1) * part] = piece[...]

    def add(step, left, right):
        total[:, step * width : (step + 1) * width] += jnp.dot(
            left, right, preferred_element_type=jnp.float32
        )

    def one(p, source):
        late = meta[LATE, p]

        @pl.when((late == 0) & (core == 0))
        def _():
            add(1, extra[p], source[(taps - 1) * rows : taps * rows])

        @pl.when((late == 1) & (core == 0))
        def _():
            add(0, extra[p, :, :half], source[taps * rows :])

        @pl.when((late == 1) & (core == 1))
        def _():
            add(0, extra[p], source[:rows])
            add(0, tiles[p, taps - 1, :, half:], source[taps * rows :])

    @pl.loop(0, tiles.shape[0])
    def _(p):
        @pl.when((meta[LATE, p] == 1) | (core == 0))
        def _():
            for slot, source in enumerate(sources):
                pl.when(meta[SLOT, p] == slot)(functools.partial(one, p, source))


def swapped_part(meta, tiles, acc, sources, pieces):
    pairs, _, rows, cols = tiles.shape
    return pl.pallas_call(
        functools.partial(swapped_kernel, len(sources)),
        out_shape=[
            pltpu.VMEM((pairs, rows, cols), tiles.dtype),
            pltpu.VMEM(acc.shape, acc.dtype),
        ],
        in_specs=[SMEM] + [VMEM] * (2 + len(sources) + len(pieces)),
        out_specs=[VMEM] * 2,
        compiler_params=SMALL,
        name="swapped_part",
    )(table(meta), held(tiles), held(acc), *[held(x) for x in sources + pieces])


def cut_kernel(start, count, *refs):
    sources, out = refs[:-1], refs[-1]
    for n, source in enumerate(sources):
        out[n * count : (n + 1) * count] = source[start : start + count]


def cut(sources, start, count):
    width = sources[0].shape[1]
    return pl.pallas_call(
        functools.partial(cut_kernel, start, count),
        out_shape=pltpu.VMEM((len(sources) * count, width), sources[0].dtype),
        in_specs=[VMEM] * len(sources),
        out_specs=VMEM,
        compiler_params=SMALL,
        name="cut",
    )(*[held(x) for x in sources])


def near_kernel(count, meta, tiles, *refs):
    sources, (total,) = refs[:count], refs[count:]
    taps, rows = tiles.shape[1:3]
    total[...] = jnp.zeros_like(total)

    def one(p, source):
        late = meta[LATE, p]
        planes = [source[k * rows : (k + 1) * rows] for k in range(taps)]
        empty = jnp.zeros_like(planes[0])
        planes = [empty] + planes + [empty]
        both = [
            jnp.concatenate(
                [
                    jnp.where(late == 1, planes[k + 2], planes[k + 1]),
                    jnp.where(late == 1, planes[k + 1], planes[k]),
                ],
                axis=1,
            )
            for k in range(taps)
        ]
        total[...] += jnp.dot(
            jnp.concatenate([tiles[p, k] for k in range(taps)], axis=1),
            jnp.concatenate(both, axis=0),
            preferred_element_type=jnp.float32,
        )

    @pl.loop(0, tiles.shape[0])
    def _(p):
        for slot, source in enumerate(sources):
            pl.when(meta[SLOT, p] == slot)(functools.partial(one, p, source))


def near_part(meta, tiles, sources):
    rows, width = tiles.shape[2], sources[0].shape[1]
    return pl.pallas_call(
        functools.partial(near_kernel, len(sources)),
        out_shape=pltpu.VMEM((rows, 2 * width), jnp.float32),
        in_specs=[SMEM] + [VMEM] * (1 + len(sources)),
        out_specs=VMEM,
        compiler_params=SMALL,
        name="near_part",
    )(table(meta), held(tiles), *[held(x) for x in sources])


def relayed_kernel(first, turns, meta, tiles, extra, acc, *refs):
    sources, (out0, out1, total, store) = refs[: 3 * turns], refs[3 * turns :]
    pairs, taps, rows = tiles.shape[:3]
    half, width = rows // 2, acc.shape[1] // 2
    held_rows = taps * rows
    block = held_rows + 3 * half
    none = 2 * turns * block
    core = meta[PLACE, 1]
    empty = jnp.zeros((half, width), store.dtype)
    for turn in range(turns):
        tops, *rests = sources[3 * turn : 3 * turn + 3]
        for n, rest in enumerate(rests):
            base = (2 * turn + n) * block
            store[base : base + HEAD] = tops[n * HEAD : (n + 1) * HEAD]
            store[base + HEAD : base + held_rows] = rest[: held_rows - HEAD]
            store[base + held_rows : base + held_rows + half] = empty
            store[base + held_rows + half : base + block - half] = rest[held_rows - HEAD :]
            store[base + block - half : base + block] = empty
    store[none:] = jnp.zeros((rows, width), store.dtype)
    total[...] = acc[...]

    def pair(a, b):
        return jnp.concatenate(
            [store[pl.ds(pl.multiple_of(at, half), rows)] for at in (a, b)], axis=1
        )

    def chunk(start):
        lefts, rights = [], []
        for i in range(start, start + CHUNK):
            p = meta[ORDER, i]
            used = i < meta[PLACE, 2]
            late = meta[LATE, p]
            base = (meta[SLOT, p] - first) * block
            early = jnp.logical_and(used, late == 0)
            after = jnp.logical_and(used, late == 1)
            ats = [jnp.where(used, base + k * rows, none) for k in range(taps)]
            last = jnp.where(jnp.logical_and(after, core == 1), base + held_rows, none)
            before = [none] + ats + [last]
            for k in range(taps):
                lefts.append(tiles[p, k])
                a = jnp.where(late == 1, before[k + 2], before[k + 1])
                b = jnp.where(late == 1, before[k + 1], before[k])
                rights.append(pair(a, b))
            lefts.append(extra[p])
            a = jnp.where(core == 0, base + held_rows + half, base)
            b = jnp.where(jnp.logical_and(early, core == 0), ats[taps - 1], none)
            rights.append(pair(jnp.where(after, a, none), b))
        total[...] += jnp.dot(
            jnp.concatenate(lefts, axis=1),
            jnp.concatenate(rights, axis=0),
            preferred_element_type=jnp.float32,
        )

    for start in range(0, pairs, CHUNK):
        pl.when(meta[PLACE, 2] > start)(functools.partial(chunk, start))
    out0[...] = total[:, :width]
    out1[...] = total[:, width:]


def relayed_part(meta, tiles, extra, acc, sources, first):
    taps, rows = tiles.shape[1:3]
    width, turns = acc.shape[1] // 2, len(sources) // 3
    store = (2 * turns * (taps * rows + 3 * rows // 2) + rows, width)
    half = pltpu.VMEM((rows, width), jnp.float32)
    room = 2 * store[0] * width + 4 * acc.size
    return pl.pallas_call(
        functools.partial(relayed_kernel, first, turns),
        out_shape=[half, half],
        in_specs=[SMEM] + [VMEM] * (3 + len(sources)),
        out_specs=[VMEM, VMEM],
        scratch_shapes=[
            pltpu.VMEM(acc.shape, acc.dtype),
            pltpu.VMEM(store, sources[0].dtype),
        ],
        compiler_params=pltpu.CompilerParams(vmem_limit_bytes=room + (4 << 20)),
        name="relayed_part",
    )(
        table(meta),
        held(tiles),
        held(extra),
        held(acc),
        *[held(x) for x in sources],
    )


def solve_rows(base, mine, other, inverse, strike, wave):
    rows, width = mine.shape
    segments = base + lax.broadcasted_iota(jnp.int32, (rows, width), 0)
    incident = jnp.where(segments == strike, wave, jnp.float32(0.0))
    rhs = (incident - (mine + other)).astype(jnp.bfloat16)
    return jnp.dot(inverse, rhs, preferred_element_type=jnp.float32).astype(
        jnp.bfloat16
    )


def first_kernel(meta, mine, other, inverse, strike, wave, out):
    out[...] = solve_rows(
        meta[PLACE, 0], mine[...], other[...], inverse[...], strike[...], wave[0:1, :]
    )


def second_kernel(meta, first, mine, other, inverse, strike, wave, out):
    out[0] = first[...]
    out[1] = solve_rows(
        meta[PLACE, 0], mine[...], other[...], inverse[...], strike[...], wave[1:2, :]
    )


def fresh_kernel(number, meta, tiles, extra, source, acc, out):
    def add(tile):
        out[...] += jnp.dot(tile, source[...], preferred_element_type=jnp.float32)

    @pl.loop(0, tiles.shape[0])
    def _(p):
        @pl.when(meta[NEWS, p] == number)
        def _():
            pl.when(meta[PLACE, 1] == 0)(lambda: add(tiles[p, 0]))
            pl.when(meta[PLACE, 1] == 1)(lambda: add(extra[p]))


def fresh_part(meta, tiles, extra, source, number, acc):
    return pl.pallas_call(
        functools.partial(fresh_kernel, number),
        out_shape=pltpu.VMEM(acc.shape, acc.dtype),
        in_specs=[SMEM] + [VMEM] * 4,
        out_specs=VMEM,
        input_output_aliases={4: 0},
        compiler_params=SMALL,
        name="fresh_part",
    )(table(meta), held(tiles), held(extra), held(source), held(acc))


def per_device(tiles, history, self_inverse, pair_src, pair_delay, strike_seg, waveform):
    sites, groups = lax.axis_size("site"), lax.axis_size("structur")
    tiles, history, inverse = tiles[0], history[0], self_inverse[0]
    pairs, taps, rows, cols = tiles.shape
    width = history.shape[2]

    kinds = ("odd", "even", "own")
    key = {(k, t): n * groups + t for n, k in enumerate(kinds) for t in range(groups)}

    def send(x, *messages):
        scenarios, grid = lax.axis_size("scenario"), sites * groups * 2
        pairs = []
        for scenario in range(scenarios):
            twin = scenario ^ 1
            for c, m in enumerate(messages):
                moves = dict(link_pairs(*m, sites, groups)) if m else {}
                for a in range(sites * groups):
                    source = scenario * grid + 2 * a + c
                    if a in moves:
                        pairs.append((source, scenario * grid + 2 * moves[a] + c))
                    elif twin < scenarios:
                        pairs.append((source, twin * grid + 2 * a + c))
        return lax.ppermute(x, ALL_AXES, pairs)

    swaps = ((("even", "odd"), ("odd", "even")), (("even", "odd"), ("odd", "even")))
    slots = [[-1] * (3 * groups) for _ in range(2)]
    for c in range(2):
        for t in range(groups):
            slots[c][key["own", t]] = t
            for n, pair in enumerate(swaps[min(t, 1)]):
                slots[c][key[pair[c], t]] = groups + 2 * t + n

    straight = [("odd", 0)]+[("own", t) for t in range(1, groups)]+[("even", 0)]
    diagonal = [(kind, t) for t in range(1, groups) for kind in ("even", "odd")]
    while len(diagonal) > len(straight):
        straight.append(diagonal.pop())
    rounds = list(itertools.zip_longest(straight, diagonal))
    news = [[-1] * (3 * groups) for _ in range(2)]
    news[1][key["own", 0]] = 0
    for n, messages in enumerate(rounds):
        for c, m in enumerate(messages):
            if m is not None:
                news[c][key[m]] = 1 + n

    planes = pl.pallas_call(
        planes_kernel,
        out_shape=pltpu.VMEM((taps * rows + rows // 2, width), history.dtype),
        in_specs=[ANY],
        out_specs=VMEM,
        scratch_shapes=[pltpu.SemaphoreType.DMA((taps + 1,))],
        compiler_params=SMALL,
        name="own_planes",
    )(far(history))
    *ends, tiles, meta = pl.pallas_call(
        functools.partial(table_kernel, slots, news, sites, groups),
        out_shape=[pltpu.VMEM((pairs // PIECES, rows, cols), tiles.dtype)] * PIECES
        + [pltpu.VMEM(tiles.shape, tiles.dtype), pltpu.SMEM((5, pairs), jnp.int32)],
        in_specs=[ANY] * 4,
        out_specs=[VMEM] * (PIECES + 1) + [SMEM],
        scratch_shapes=[
            pltpu.SMEM((1, pairs), jnp.int32),
            pltpu.SMEM((1, pairs), jnp.int32),
            pltpu.SemaphoreType.DMA((3 + pairs,)),
        ],
        compiler_params=SMALL,
        name="table",
    )(far(pair_src), far(pair_delay), far(tiles), planes)

    own = [planes] + [send(planes, *[("own", t)] * 2) for t in range(1, groups)]
    partners = [send(planes, *[(kind, 0) for kind in pair]) for pair in swaps[0]]
    tops = cut(partners, 0, HEAD)
    relayed = []
    for x in own[1:]:
        rest = cut([x], HEAD, x.shape[0] - HEAD)
        relayed.append(send(tops, *[("own", len(relayed) // 3 + 1)] * 2))
        relayed += [send(rest, *[(kind, 0) for kind in pair]) for pair in swaps[1]]
    pieces = [swap_cores(x) for x in ends]

    near = own + partners
    acc = near_part(meta, tiles, near)
    extra, acc = swapped_part(meta, tiles, acc, near, pieces)
    mine0, mine1 = relayed_part(meta, tiles, extra, acc, relayed, groups + 2)

    strike, inverse, wave = held(strike_seg[None, :]), held(inverse), held(waveform)
    current0 = pl.pallas_call(
        first_kernel,
        out_shape=pltpu.VMEM((rows, width), jnp.bfloat16),
        in_specs=[SMEM] + [VMEM] * 5,
        out_specs=VMEM,
        compiler_params=SMALL,
        name="first_currents",
    )(table(meta), held(mine0), held(swap_cores(mine0)), inverse, strike, wave)

    fresh = [send(current0, *messages) for messages in rounds]
    for number, block in enumerate([current0] + fresh):
        mine1 = fresh_part(meta, tiles, extra, block, number, mine1)

    currents = pl.pallas_call(
        second_kernel,
        out_shape=jax.ShapeDtypeStruct((2, rows, width), jnp.bfloat16),
        in_specs=[SMEM] + [VMEM] * 6,
        out_specs=VMEM,
        compiler_params=SMALL,
        name="second_currents",
    )(
        table(meta),
        held(current0),
        held(mine1),
        held(swap_cores(mine1)),
        inverse,
        strike,
        wave,
    )
    return currents[None]


def solution(mesh):
    in_specs = (
        P(("site", "structur"), None, "sub", None, None),
        P(("scenario", "site", "structur"), None, None, None),
        P(("site", "structur"), None, None),
        P(("site", "structur"), None),
        P(("site", "structur"), None),
        P("scenario"),
        P("scenario", None),
    )
    out_specs = P(("scenario", "site", "structur"), None, None, None)
    return jax.shard_map(
        per_device, mesh=mesh, in_specs=in_specs, out_specs=out_specs, check_vma=False
    )
```

```python
import functools
import itertools

import jax
import jax.numpy as jnp
from jax import lax
from jax.experimental import pallas as pl
from jax.experimental.pallas import tpu as pltpu
from jax.sharding import PartitionSpec as P

GRID_AXES = ("site", "structur", "sub")
ALL_AXES = ("scenario",) + GRID_AXES
SMEM = pl.BlockSpec(memory_space=pltpu.SMEM)
VMEM = pl.BlockSpec(memory_space=pltpu.VMEM)
ANY = pl.BlockSpec(memory_space=pl.ANY)
SMALL = pltpu.CompilerParams(vmem_limit_bytes=4 << 20)

SLOT, LATE, NEWS, ORDER, PLACE = range(5)
CHUNK = 2
PIECES = 4
HEAD = 96


def held(x):
    return pltpu.with_memory_space_constraint(x, pltpu.VMEM)


def far(x):
    return pltpu.with_memory_space_constraint(x, pltpu.HBM)


def table(x):
    return pltpu.with_memory_space_constraint(x, pltpu.SMEM)


def partner_site(site, kind, sites):
    other = site ^ 1 if kind == "even" else (site + 1 if site % 2 else site - 1)
    return other if 0 <= other < sites else None


def link_pairs(kind, turn, sites, groups):
    pairs = []
    for site in range(sites):
        to_site = site if kind == "own" else partner_site(site, kind, sites)
        if to_site is None:
            continue
        for member in range(groups):
            pairs.append(
                (site * groups + member, to_site * groups + (member - turn) % groups)
            )
    return pairs


def swap_cores(x):
    return lax.ppermute(x, "sub", [(0, 1), (1, 0)])


def planes_kernel(history, planes, sem):
    core = lax.axis_index("sub")
    count, rows, _ = history.shape
    taps, half = count // 2, rows // 2
    copies = [
        pltpu.make_async_copy(
            history.at[core * taps + n], planes.at[pl.ds(n * rows, rows)], sem.at[n]
        )
        for n in range(taps)
    ]
    copies.append(
        pltpu.make_async_copy(
            history.at[count - 1, pl.ds(core * half, half)],
            planes.at[pl.ds(taps * rows, half)],
            sem.at[taps],
        )
    )
    for copy in copies:
        copy.start()
    for copy in copies:
        copy.wait()


def table_kernel(slots, news, sites, groups, *refs):
    src, delay, tiles, after = refs[:4]
    *ends, whole, meta, src_buf, delay_buf, sem = refs[4:]
    part = ends[0].shape[0]
    site, member, core = (lax.axis_index(a) for a in GRID_AXES)
    rows = tiles.shape[2]
    copies = [
        pltpu.make_async_copy(src, src_buf, sem.at[0]),
        pltpu.make_async_copy(delay, delay_buf, sem.at[1]),
        pltpu.make_async_copy(tiles, whole, sem.at[2]),
    ]
    for copy in copies:
        copy.start()
    copies[0].wait()
    copies[1].wait()
    last = tiles.shape[1] - 1
    for p in range(src.shape[1]):
        copies.append(
            pltpu.make_async_copy(
                tiles.at[p, jnp.where(delay_buf[0, p] == 1, 0, last)],
                ends[p // part].at[p % part],
                sem.at[3 + p],
            )
        )
        copies[-1].start()
    even_step = jnp.where(site % 2 == 0, 1, -1)
    ahead = jnp.int32(0)
    behind = jnp.int32(src.shape[1])
    for p in range(src.shape[1]):
        value, wait = src_buf[0, p], delay_buf[0, p]
        turn = (value % groups - member + groups) % groups
        dist = value // groups - site
        kind = jnp.where(dist == 0, 2, jnp.where(dist == even_step, 1, 0))
        key = kind * groups + turn
        slot, fresh = jnp.int32(-1), jnp.int32(-1)
        for n in range(3 * groups):
            mine = [jnp.where(core == 0, t[0][n], t[1][n]) for t in (slots, news)]
            slot = jnp.where(key == n, mine[0], slot)
            fresh = jnp.where(key == n, mine[1], fresh)
        meta[SLOT, p] = slot
        meta[LATE, p] = wait - 1
        meta[NEWS, p] = jnp.where(wait == 1, fresh, -1)
        relayed = slot >= groups + 2
        behind = behind - jnp.where(relayed, 0, 1)
        meta[ORDER, jnp.where(relayed, ahead, behind)] = p
        ahead = ahead + jnp.where(relayed, 1, 0)
        meta[PLACE, p] = core
    meta[PLACE, 0] = (site * groups + member) * rows
    meta[PLACE, 2] = ahead
    for copy in copies[2:]:
        copy.wait()


def swapped_kernel(count, meta, tiles, acc, *refs):
    sources, pieces = refs[:count], refs[count:-2]
    extra, total = refs[-2:]
    part = pieces[0].shape[0]
    taps, rows = tiles.shape[1:3]
    half, width = rows // 2, sources[0].shape[1]
    core = meta[PLACE, 1]
    total[...] = acc[...]
    for n, piece in enumerate(pieces):
        extra[n * part : (n + 1) * part] = piece[...]

    def add(step, left, right):
        total[:, step * width : (step + 1) * width] += jnp.dot(
            left, right, preferred_element_type=jnp.float32
        )

    def one(p, source):
        late = meta[LATE, p]

        @pl.when((late == 0) & (core == 0))
        def _():
            add(1, extra[p], source[(taps - 1) * rows : taps * rows])

        @pl.when((late == 1) & (core == 0))
        def _():
            add(0, extra[p, :, :half], source[taps * rows :])

        @pl.when((late == 1) & (core == 1))
        def _():
            add(0, extra[p], source[:rows])
            add(0, tiles[p, taps - 1, :, half:], source[taps * rows :])

    @pl.loop(0, tiles.shape[0])
    def _(p):
        @pl.when((meta[LATE, p] == 1) | (core == 0))
        def _():
            for slot, source in enumerate(sources):
                pl.when(meta[SLOT, p] == slot)(functools.partial(one, p, source))


def swapped_part(meta, tiles, acc, sources, pieces):
    pairs, _, rows, cols = tiles.shape
    return pl.pallas_call(
        functools.partial(swapped_kernel, len(sources)),
        out_shape=[
            pltpu.VMEM((pairs, rows, cols), tiles.dtype),
            pltpu.VMEM(acc.shape, acc.dtype),
        ],
        in_specs=[SMEM] + [VMEM] * (2 + len(sources) + len(pieces)),
        out_specs=[VMEM] * 2,
        compiler_params=SMALL,
        name="swapped_part",
    )(table(meta), held(tiles), held(acc), *[held(x) for x in sources + pieces])


def cut_kernel(start, count, *refs):
    sources, out = refs[:-1], refs[-1]
    for n, source in enumerate(sources):
        out[n * count : (n + 1) * count] = source[start : start + count]


def cut(sources, start, count):
    width = sources[0].shape[1]
    return pl.pallas_call(
        functools.partial(cut_kernel, start, count),
        out_shape=pltpu.VMEM((len(sources) * count, width), sources[0].dtype),
        in_specs=[VMEM] * len(sources),
        out_specs=VMEM,
        compiler_params=SMALL,
        name="cut",
    )(*[held(x) for x in sources])


def near_kernel(count, meta, tiles, *refs):
    sources, (total,) = refs[:count], refs[count:]
    taps, rows = tiles.shape[1:3]
    total[...] = jnp.zeros_like(total)

    def one(p, source):
        late = meta[LATE, p]
        planes = [source[k * rows : (k + 1) * rows] for k in range(taps)]
        empty = jnp.zeros_like(planes[0])
        planes = [empty] + planes + [empty]
        both = [
            jnp.concatenate(
                [
                    jnp.where(late == 1, planes[k + 2], planes[k + 1]),
                    jnp.where(late == 1, planes[k + 1], planes[k]),
                ],
                axis=1,
            )
            for k in range(taps)
        ]
        total[...] += jnp.dot(
            jnp.concatenate([tiles[p, k] for k in range(taps)], axis=1),
            jnp.concatenate(both, axis=0),
            preferred_element_type=jnp.float32,
        )

    @pl.loop(0, tiles.shape[0])
    def _(p):
        for slot, source in enumerate(sources):
            pl.when(meta[SLOT, p] == slot)(functools.partial(one, p, source))


def near_part(meta, tiles, sources):
    rows, width = tiles.shape[2], sources[0].shape[1]
    return pl.pallas_call(
        functools.partial(near_kernel, len(sources)),
        out_shape=pltpu.VMEM((rows, 2 * width), jnp.float32),
        in_specs=[SMEM] + [VMEM] * (1 + len(sources)),
        out_specs=VMEM,
        compiler_params=SMALL,
        name="near_part",
    )(table(meta), held(tiles), *[held(x) for x in sources])


def relayed_kernel(first, turns, meta, tiles, extra, acc, *refs):
    sources, (out0, out1, store) = refs[: 3 * turns], refs[3 * turns :]
    pairs, taps, rows = tiles.shape[:3]
    half, width = rows // 2, acc.shape[1] // 2
    held_rows = taps * rows
    block = held_rows + 3 * half
    none = 2 * turns * block
    core = meta[PLACE, 1]
    empty = jnp.zeros((half, width), store.dtype)
    for turn in range(turns):
        tops, *rests = sources[3 * turn : 3 * turn + 3]
        for n, rest in enumerate(rests):
            base = (2 * turn + n) * block
            store[base : base + HEAD] = tops[n * HEAD : (n + 1) * HEAD]
            store[base + HEAD : base + held_rows] = rest[: held_rows - HEAD]
            store[base + held_rows : base + held_rows + half] = empty
            store[base + held_rows + half : base + block - half] = rest[held_rows - HEAD :]
            store[base + block - half : base + block] = empty
    store[none:] = jnp.zeros((rows, width), store.dtype)
    out0[...] = acc[:, :width]
    out1[...] = acc[:, width:]

    def pair(a, b):
        return jnp.concatenate(
            [store[pl.ds(pl.multiple_of(at, half), rows)] for at in (a, b)], axis=1
        )

    def chunk(start):
        lefts, rights = [], []
        for i in range(start, start + CHUNK):
            p = meta[ORDER, i]
            used = i < meta[PLACE, 2]
            late = meta[LATE, p]
            base = (meta[SLOT, p] - first) * block
            early = jnp.logical_and(used, late == 0)
            after = jnp.logical_and(used, late == 1)
            ats = [jnp.where(used, base + k * rows, none) for k in range(taps)]
            last = jnp.where(jnp.logical_and(after, core == 1), base + held_rows, none)
            before = [none] + ats + [last]
            for k in range(taps):
                lefts.append(tiles[p, k])
                a = jnp.where(late == 1, before[k + 2], before[k + 1])
                b = jnp.where(late == 1, before[k + 1], before[k])
                rights.append(pair(a, b))
            lefts.append(extra[p])
            a = jnp.where(core == 0, base + held_rows + half, base)
            b = jnp.where(jnp.logical_and(early, core == 0), ats[taps - 1], none)
            rights.append(pair(jnp.where(after, a, none), b))
        sums = jnp.dot(
            jnp.concatenate(lefts, axis=1),
            jnp.concatenate(rights, axis=0),
            preferred_element_type=jnp.float32,
        )
        out0[...] += sums[:, :width]
        out1[...] += sums[:, width:]

    for start in range(0, pairs, CHUNK):
        pl.when(meta[PLACE, 2] > start)(functools.partial(chunk, start))


def relayed_part(meta, tiles, extra, acc, sources, first):
    taps, rows = tiles.shape[1:3]
    width, turns = acc.shape[1] // 2, len(sources) // 3
    store = (2 * turns * (taps * rows + 3 * rows // 2) + rows, width)
    half = pltpu.VMEM((rows, width), jnp.float32)
    room = 2 * store[0] * width + 4 * acc.size
    return pl.pallas_call(
        functools.partial(relayed_kernel, first, turns),
        out_shape=[half, half],
        in_specs=[SMEM] + [VMEM] * (3 + len(sources)),
        out_specs=[VMEM, VMEM],
        scratch_shapes=[pltpu.VMEM(store, sources[0].dtype)],
        compiler_params=pltpu.CompilerParams(vmem_limit_bytes=room + (4 << 20)),
        name="relayed_part",
    )(
        table(meta),
        held(tiles),
        held(extra),
        held(acc),
        *[held(x) for x in sources],
    )


def solve_rows(base, mine, other, inverse, strike, wave):
    rows, width = mine.shape
    segments = base + lax.broadcasted_iota(jnp.int32, (rows, width), 0)
    incident = jnp.where(segments == strike, wave, jnp.float32(0.0))
    rhs = (incident - (mine + other)).astype(jnp.bfloat16)
    return jnp.dot(inverse, rhs, preferred_element_type=jnp.float32).astype(
        jnp.bfloat16
    )


def first_kernel(meta, mine, other, inverse, strike, wave, out):
    out[...] = solve_rows(
        meta[PLACE, 0], mine[...], other[...], inverse[...], strike[...], wave[0:1, :]
    )


def second_kernel(meta, first, mine, other, inverse, strike, wave, out):
    out[0] = first[...]
    out[1] = solve_rows(
        meta[PLACE, 0], mine[...], other[...], inverse[...], strike[...], wave[1:2, :]
    )


def fresh_kernel(number, meta, tiles, extra, source, acc, out):
    def add(tile):
        out[...] += jnp.dot(tile, source[...], preferred_element_type=jnp.float32)

    @pl.loop(0, tiles.shape[0])
    def _(p):
        @pl.when(meta[NEWS, p] == number)
        def _():
            pl.when(meta[PLACE, 1] == 0)(lambda: add(tiles[p, 0]))
            pl.when(meta[PLACE, 1] == 1)(lambda: add(extra[p]))


def fresh_part(meta, tiles, extra, source, number, acc):
    return pl.pallas_call(
        functools.partial(fresh_kernel, number),
        out_shape=pltpu.VMEM(acc.shape, acc.dtype),
        in_specs=[SMEM] + [VMEM] * 4,
        out_specs=VMEM,
        input_output_aliases={4: 0},
        compiler_params=SMALL,
        name="fresh_part",
    )(table(meta), held(tiles), held(extra), held(source), held(acc))


def per_device(tiles, history, self_inverse, pair_src, pair_delay, strike_seg, waveform):
    sites, groups = lax.axis_size("site"), lax.axis_size("structur")
    tiles, history, inverse = tiles[0], history[0], self_inverse[0]
    pairs, taps, rows, cols = tiles.shape
    width = history.shape[2]

    kinds = ("odd", "even", "own")
    key = {(k, t): n * groups + t for n, k in enumerate(kinds) for t in range(groups)}

    def send(x, *messages):
        scenarios, grid = lax.axis_size("scenario"), sites * groups * 2
        pairs = []
        for scenario in range(scenarios):
            twin = scenario ^ 1
            for c, m in enumerate(messages):
                moves = dict(link_pairs(*m, sites, groups)) if m else {}
                for a in range(sites * groups):
                    source = scenario * grid + 2 * a + c
                    if a in moves:
                        pairs.append((source, scenario * grid + 2 * moves[a] + c))
                    elif twin < scenarios:
                        pairs.append((source, twin * grid + 2 * a + c))
        return lax.ppermute(x, ALL_AXES, pairs)

    swaps = ((("even", "odd"), ("odd", "even")), (("even", "odd"), ("odd", "even")))
    slots = [[-1] * (3 * groups) for _ in range(2)]
    for c in range(2):
        for t in range(groups):
            slots[c][key["own", t]] = t
            for n, pair in enumerate(swaps[min(t, 1)]):
                slots[c][key[pair[c], t]] = groups + 2 * t + n

    straight = [("odd", 0)]+[("own", t) for t in range(1, groups)]+[("even", 0)]
    diagonal = [(kind, t) for t in range(1, groups) for kind in ("even", "odd")]
    while len(diagonal) > len(straight):
        straight.append(diagonal.pop())
    rounds = list(itertools.zip_longest(straight, diagonal))
    news = [[-1] * (3 * groups) for _ in range(2)]
    news[1][key["own", 0]] = 0
    for n, messages in enumerate(rounds):
        for c, m in enumerate(messages):
            if m is not None:
                news[c][key[m]] = 1 + n

    planes = pl.pallas_call(
        planes_kernel,
        out_shape=pltpu.VMEM((taps * rows + rows // 2, width), history.dtype),
        in_specs=[ANY],
        out_specs=VMEM,
        scratch_shapes=[pltpu.SemaphoreType.DMA((taps + 1,))],
        compiler_params=SMALL,
        name="own_planes",
    )(far(history))
    *ends, tiles, meta = pl.pallas_call(
        functools.partial(table_kernel, slots, news, sites, groups),
        out_shape=[pltpu.VMEM((pairs // PIECES, rows, cols), tiles.dtype)] * PIECES
        + [pltpu.VMEM(tiles.shape, tiles.dtype), pltpu.SMEM((5, pairs), jnp.int32)],
        in_specs=[ANY] * 4,
        out_specs=[VMEM] * (PIECES + 1) + [SMEM],
        scratch_shapes=[
            pltpu.SMEM((1, pairs), jnp.int32),
            pltpu.SMEM((1, pairs), jnp.int32),
            pltpu.SemaphoreType.DMA((3 + pairs,)),
        ],
        compiler_params=SMALL,
        name="table",
    )(far(pair_src), far(pair_delay), far(tiles), planes)

    own = [planes] + [send(planes, *[("own", t)] * 2) for t in range(1, groups)]
    partners = [send(planes, *[(kind, 0) for kind in pair]) for pair in swaps[0]]
    tops = cut(partners, 0, HEAD)
    relayed = []
    for x in own[1:]:
        rest = cut([x], HEAD, x.shape[0] - HEAD)
        relayed.append(send(tops, *[("own", len(relayed) // 3 + 1)] * 2))
        relayed += [send(rest, *[(kind, 0) for kind in pair]) for pair in swaps[1]]
    pieces = [swap_cores(x) for x in ends]

    near = own + partners
    acc = near_part(meta, tiles, near)
    extra, acc = swapped_part(meta, tiles, acc, near, pieces)
    mine0, mine1 = relayed_part(meta, tiles, extra, acc, relayed, groups + 2)

    strike, inverse, wave = held(strike_seg[None, :]), held(inverse), held(waveform)
    current0 = pl.pallas_call(
        first_kernel,
        out_shape=pltpu.VMEM((rows, width), jnp.bfloat16),
        in_specs=[SMEM] + [VMEM] * 5,
        out_specs=VMEM,
        compiler_params=SMALL,
        name="first_currents",
    )(table(meta), held(mine0), held(swap_cores(mine0)), inverse, strike, wave)

    fresh = [send(current0, *messages) for messages in rounds]
    for number, block in enumerate([current0] + fresh):
        mine1 = fresh_part(meta, tiles, extra, block, number, mine1)

    currents = pl.pallas_call(
        second_kernel,
        out_shape=jax.ShapeDtypeStruct((2, rows, width), jnp.bfloat16),
        in_specs=[SMEM] + [VMEM] * 6,
        out_specs=VMEM,
        compiler_params=SMALL,
        name="second_currents",
    )(
        table(meta),
        held(current0),
        held(mine1),
        held(swap_cores(mine1)),
        inverse,
        strike,
        wave,
    )
    return currents[None]


def solution(mesh):
    in_specs = (
        P(("site", "structur"), None, "sub", None, None),
        P(("scenario", "site", "structur"), None, None, None),
        P(("site", "structur"), None, None),
        P(("site", "structur"), None),
        P(("site", "structur"), None),
        P("scenario"),
        P("scenario", None),
    )
    out_specs = P(("scenario", "site", "structur"), None, None, None)
    return jax.shard_map(
        per_device, mesh=mesh, in_specs=in_specs, out_specs=out_specs, check_vma=False
    )
```
